512 devices in a mesh: tm: 8 (over y), pts: 64 (over x, z, core).
Axes of the slice: x: 4, y: 8, z: 8, core: 2. Of those that a mesh axis runs over, the one named last changes fastest.
Arguments:
- precip: float32 [2048, 65536], P('tm', 'pts'), may hold values from -150 to 300, as said below
- thresholds: float32 [64], replicated, may hold values from -1 to 5
- bin_index: int32 [65536], P('pts'), may hold values from 0 to 63
- test_matrix: float32 [2048, 256], P('tm'), may hold values from -0.125 to 0.125
Outputs:
- basis: float32 [65536, 256], P(('pts', 'tm'))
- factor: float32 [256, 256], replicated
The draws below stay inside these ranges and needn't reach their ends.
Inputs may be any that keep to these rules, and one draw needn't show every extreme that they name: `precip`: precipitation records.
All inputs are finite; a program needn't handle non-finite values.
Results may differ from the reference program's by a relative error of at most 0.0003.
Values sent between devices are 32-bit elements; how exact they have to be, the bound alone decides.
A program may use at most 64 MiB of HBM per device.

```python
import math
import jax
import jax.numpy as jnp
from jax import lax

K = 256
HARM = 8
NBINS = 64
DAYS = 2048
POINTS = 65536


def draw_precip(key, part):
    keys = jax.random.split(key, 5)
    position = jnp.arange(POINTS, dtype=jnp.float32) / max(POINTS - 1, 1)
    spread = jnp.exp(jax.random.uniform(keys[0], (POINTS,), minval=0.0, maxval=math.log(10.0)))
    scaling = spread * jnp.exp(math.log(3.0) * position)
    amplitude = jax.random.uniform(keys[1], (POINTS,), minval=0.5, maxval=2.0)
    shifted = jax.random.uniform(keys[2], (POINTS,), minval=-math.pi, maxval=math.pi)
    day_number = jnp.arange(DAYS, dtype=jnp.float32)[:, None]
    season = amplitude[None, :] * jnp.cos(2.0 * math.pi / 365.25 * day_number + shifted[None, :])
    baseline = jax.random.uniform(keys[3], (POINTS,), minval=1.0, maxval=3.0)
    noise = jnp.clip(jax.random.normal(keys[4], (DAYS, POINTS), jnp.float32), -4.0, 4.0)
    values = scaling[None, :] * (baseline[None, :] + season + noise)
    return values.astype(jnp.float32)


def with_ends(result, rng, least, high):
    longest = result.shape.index(max(result.shape))
    spots = []
    for shift in (0, 1):
        where = [jax.random.randint(jax.random.fold_in(rng, axis), (), 0, length) for axis, length in enumerate(result.shape)]
        where[longest] = (where[longest] + shift) % result.shape[longest]
        spots.append(tuple(where))
    return result.at[spots[0]].set(least).at[spots[1]].set(high)


def block_scale(rng, extent, pieces, least, high):
    gain = 1.0
    for dim, parts in pieces:
        heights = jax.random.uniform(jax.random.fold_in(jax.random.fold_in(rng, 6), dim), (parts,), jnp.float32, least / len(pieces), high / len(pieces))
        gain = gain * jnp.repeat(jnp.exp(heights), extent[dim] // parts).reshape((-1,) + (1,) * (len(extent) - 1 - dim))
    return gain


def gaussian(own_key, shape, width, bound, cuts=(), kind=jnp.bfloat16):
    array = width * jax.random.normal(own_key, shape, jnp.float32)
    if cuts:
        array = array * block_scale(own_key, shape, cuts, -0.22, 0.18)
    return jnp.clip(array, -bound, bound).astype(kind)


def setup_inputs(seed: int = 0) -> dict:
    key_of = jax.random.split(jax.random.key(seed), 5)
    return {
        "precip": draw_precip(jax.random.fold_in(key_of[4], 71), 0),
        "thresholds": jnp.clip(jax.random.uniform(key_of[1], (NBINS,), jnp.float32, -1.0, 5.0), -1.0, 5.0),
        "bin_index": with_ends(jax.random.randint(key_of[2], (POINTS,), 0, NBINS), jax.random.fold_in(key_of[2], 1), 0, NBINS - 1).astype(jnp.int32),
        "test_matrix": gaussian(key_of[3], (DAYS, K), DAYS ** -0.5, 0.125, ((0, 8),), jnp.float32),
    }


year_days = 365.25

def harmonic_table(day_number):
    phase_base = day_number.astype(jnp.float32)
    columns = [jnp.ones_like(phase_base)]
    for order in range(1, HARM + 1):
        phase = 2.0 * math.pi * order / year_days * phase_base
        columns.append(jnp.cos(phase))
        columns.append(jnp.sin(phase))
    return jnp.stack(columns, 0)

def normal_solve(factor_low, values):
    forward = lax.linalg.triangular_solve(factor_low, values, left_side=True, lower=True)
    return lax.linalg.triangular_solve(factor_low, forward, left_side=True, lower=True, transpose_a=True)

def reference(precip, thresholds, bin_index, test_matrix):
    highest = lax.Precision.HIGHEST
    harmonic_cols = harmonic_table(jnp.arange(DAYS, dtype=jnp.int32))
    normal = jnp.dot(harmonic_cols, harmonic_cols.T, precision=highest)
    projections = jnp.dot(harmonic_cols, precip, precision=highest)
    coefficients = normal_solve(jnp.linalg.cholesky(normal), projections)
    anomaly = precip - jnp.dot(harmonic_cols.T, coefficients, precision=highest)
    level = thresholds[bin_index]
    excess = jnp.maximum(anomaly - level[None, :], 0.0)
    sketch = lax.dot_general(excess, test_matrix, (((0,), (0,)), ((), ())), precision=highest)
    cross = jnp.dot(sketch.T, sketch, precision=highest) / POINTS
    lower = jnp.linalg.cholesky(cross)
    basis = lax.linalg.triangular_solve(lower, sketch, left_side=False, lower=True, transpose_a=True)
    return (basis, lower.T)
```

```python
import functools
import math

import jax
import jax.numpy as jnp
import numpy as np
from jax import lax
from jax.experimental import pallas as pl
from jax.experimental.pallas import tpu as pltpu
from jax.sharding import Mesh
from jax.sharding import PartitionSpec as P

HARM = 8
YEAR_DAYS = 365.25
ROWS = 24
PTS = ("pts_0", "pts_1", "pts_2")
PTS_TM = ("pts_0", "pts_1", "pts_2", "tm")
MESH = pl.DeviceIdType.MESH
HIGHEST = lax.Precision.HIGHEST


def harmonic_basis(days):
    day = np.arange(days, dtype=np.float32)
    columns = [np.ones(days)]
    for order in range(1, HARM + 1):
        phase = (np.float32(2.0 * math.pi * order / YEAR_DAYS) * day).astype(np.float64)
        columns += [np.cos(phase), np.sin(phase)]
    table = np.stack(columns)
    return np.linalg.solve(np.linalg.cholesky(table @ table.T), table)


def dot(a, b, dims):
    return lax.dot_general(
        a, b, (dims, ((), ())), precision=HIGHEST, preferred_element_type=jnp.float32
    )


def gather_kernel(
    scale,
    precip,
    table,
    test,
    bins,
    thresholds,
    sketch_out,
    cross_out,
    *scratch,
):
    (
        test_t,
        proj_out,
        proj_in,
        coef,
        level,
        sketch,
        ring,
        cross,
        core_in,
        y_in,
        z_in,
        x_in,
        total,
        proj_sem,
        coef_sem,
        ring_sem,
        core_sem,
        y_sem,
        z_sem,
        x_sem,
        gather_sem,
        join_sem,
    ) = scratch
    y = lax.axis_index("tm")
    x = lax.axis_index("pts_0")
    z = lax.axis_index("pts_1")
    c = lax.axis_index("pts_2")
    n_y, n_x, n_z = (lax.axis_size(a) for a in ("tm", "pts_0", "pts_1"))
    sends = []

    def send(src, dst, sem, device):
        copy = pltpu.make_async_remote_copy(
            src_ref=src,
            dst_ref=dst,
            send_sem=sem.at[0],
            recv_sem=sem.at[1],
            device_id=device,
            device_id_type=MESH,
        )
        copy.start()
        sends.append(copy)
        return copy

    y_at = lambda o: lax.rem(y + o + n_y, n_y)
    x_at = lambda o: lax.rem(x + o + n_x, n_x)
    z_at = lambda o: lax.rem(z + o + n_z, n_z)

    barrier = pltpu.get_barrier_semaphore()
    others = [{"tm": y_at(o)} for o in range(1, n_y)]
    others += [{"pts_0": x_at(o)} for o in range(1, n_x)]
    others += [{"pts_1": z_at(o)} for o in range(1, n_z)]
    others += [{"pts_2": 1 - c}]
    for other in others:
        pl.semaphore_signal(barrier, inc=1, device_id=other, device_id_type=MESH)

    mine = table[y]
    proj = dot(mine, precip[...], ((1,), (0,)))
    for r in range(n_y):
        proj_out[r] = proj[:, 128 * r : 128 * (r + 1)]
    pl.semaphore_wait(barrier, len(others))
    arrivals = []
    for o in [4, 3, 5, 2, 6, 1, 7]:
        arrivals.append(send(proj_out.at[y_at(o)], proj_in.at[o], proj_sem.at[o], {"tm": y_at(o)}))
    test_t[...] = test[...].T
    found = bins[...]
    value = jnp.zeros(found.shape, jnp.float32)
    for k in range(thresholds.shape[0]):
        value = jnp.where(found == k, thresholds[k], value)
    level[...] = value
    for copy in arrivals:
        copy.wait_recv()
    own = proj_out[y]
    for o in range(1, n_y):
        own = own + proj_in[o]
    coef[y] = own
    arrivals = []
    for o in [4, 3, 5, 2, 6, 1, 7]:
        arrivals.append(send(coef.at[y], coef.at[y], coef_sem.at[o], {"tm": y_at(o)}))
    for copy in arrivals:
        copy.wait_recv()

    def partial(o):
        r = y_at(o)
        fit = dot(mine, coef[r], ((0,), (0,)))
        data = precip[:, pl.ds(pl.multiple_of(128 * r, 128), 128)]
        excess = jnp.maximum(data - fit - level[pl.ds(r, 1), :], 0.0)
        sketch[o % n_y] = dot(test_t[...], excess, ((1,), (0,)))

    n_p = ring.shape[1] // 2
    piece = 128 // n_p

    def chain(way, q, step):
        hops = 4 if (q < n_p) == (way == 0) else 3
        if step > hops:
            return None
        o = hops + 1 - step
        return o if way == 0 else -o

    def rows_of(q):
        return pl.ds(q * piece, piece)

    def hop(way, q, step):
        o = chain(way, q, step) % n_y
        src = sketch.at[o, rows_of(q)] if step == 1 else ring.at[way, q, step - 2]
        return send(
            src,
            ring.at[way, q, step - 1],
            ring_sem.at[way, q, step - 1],
            {"tm": y_at(1 if way == 0 else -1)},
        )

    order = [(w, q) for q in range(n_p) for w in (0, 1)]
    long = [(w, q if w == 0 else q + n_p) for w, q in order]
    short = [(w, q + n_p if w == 0 else q) for w, q in order]
    moving = {}
    partial(4)
    for w, q in long:
        moving[w, q] = hop(w, q, 1)
    partial(3)
    for w, q in short:
        if w == 0:
            moving[w, q] = hop(w, q, 1)
    partial(-3)
    for w, q in short:
        if w == 1:
            moving[w, q] = hop(w, q, 1)
    partial(2)
    partial(-2)
    for step in (2, 3, 4):
        for w, q in long + short:
            o = chain(w, q, step)
            if o is None:
                continue
            moving[w, q].wait_recv()
            ring[w, q, step - 2] += sketch[o % n_y, rows_of(q)]
            moving[w, q] = hop(w, q, step)
        if step == 2:
            partial(1)
            partial(-1)
            partial(0)
    for q in range(2 * n_p):
        value = sketch[0, rows_of(q)]
        for w in (0, 1):
            hops = 4 if (w, q) in long else 3
            moving[w, q].wait_recv()
            value = value + ring[w, q, hops - 1]
        sketch_out[rows_of(q)] = value

    upper = sketch_out[:128]
    lower = sketch_out[128:]
    cross[:128] = dot(upper, upper, ((1,), (1,))) * scale
    cross[128:256] = dot(lower, upper, ((1,), (1,))) * scale
    cross[256:] = dot(lower, lower, ((1,), (1,))) * scale
    half = cross.shape[0] // 2
    part = half // n_y
    copy = send(
        cross.at[pl.ds(pl.multiple_of((1 - c) * half, 8), half)], core_in, core_sem, {"pts_2": 1 - c}
    )
    copy.wait_recv()
    core_in[...] += cross[pl.ds(pl.multiple_of(c * half, 8), half)]
    arrivals = []
    for o in [4, 3, 5, 2, 6, 1, 7]:
        arrivals.append(
            send(
                core_in.at[pl.ds(pl.multiple_of(y_at(o) * part, 8), part)],
                y_in.at[o],
                y_sem.at[o],
                {"tm": y_at(o)},
            )
        )
    for copy in arrivals:
        copy.wait_recv()
    own = core_in[pl.ds(pl.multiple_of(y * part, 8), part)]
    for o in range(1, n_y):
        own = own + y_in[o]
    z_in[z] = own
    arrivals = []
    for o in [4, 3, 5, 2, 6, 1, 7]:
        arrivals.append(send(z_in.at[z], z_in.at[z], z_sem.at[o], {"pts_1": z_at(o)}))
    for copy in arrivals:
        copy.wait_recv()
    own = z_in[0]
    for o in range(1, n_z):
        own = own + z_in[o]
    x_in[x] = own
    arrivals = []
    for o in [2, 1, 3]:
        arrivals.append(send(x_in.at[x], x_in.at[x], x_sem.at[o], {"pts_0": x_at(o)}))
    for copy in arrivals:
        copy.wait_recv()
    own = x_in[0]
    for o in range(1, n_x):
        own = own + x_in[o]
    place = pl.ds(pl.multiple_of(c * half + y * part, 8), part)
    total[place] = own
    arrivals = []
    for o in [4, 3, 5, 2, 6, 1, 7]:
        arrivals.append(send(total.at[place], total.at[place], gather_sem.at[o], {"tm": y_at(o)}))
    for copy in arrivals:
        copy.wait_recv()
    place = pl.ds(pl.multiple_of(c * half, 8), half)
    send(total.at[place], total.at[place], join_sem, {"pts_2": 1 - c}).wait_recv()
    cross_out[...] = total[...]
    for copy in sends:
        copy.wait_send()


PIECES = 2


def gathered(precip, table, test, bins, thresholds, points_total):
    vmem = pl.BlockSpec(memory_space=pltpu.VMEM)
    smem = pl.BlockSpec(memory_space=pltpu.SMEM)
    f32 = jnp.float32
    dma = pltpu.SemaphoreType.DMA
    half = 192
    part = 24
    return pl.pallas_call(
        functools.partial(gather_kernel, 1.0 / points_total),
        out_shape=(
            jax.ShapeDtypeStruct((256, 128), f32),
            jax.ShapeDtypeStruct((384, 128), f32),
        ),
        in_specs=[vmem, vmem, vmem, vmem, smem],
        out_specs=(vmem, vmem),
        scratch_shapes=[
            pltpu.VMEM((256, 256), f32),
            pltpu.VMEM((8, ROWS, 128), f32),
            pltpu.VMEM((8, ROWS, 128), f32),
            pltpu.VMEM((8, ROWS, 128), f32),
            pltpu.VMEM((8, 128), f32),
            pltpu.VMEM((8, 256, 128), f32),
            pltpu.VMEM((2, 2 * PIECES, 4, 128 // PIECES, 128), f32),
            pltpu.VMEM((384, 128), f32),
            pltpu.VMEM((half, 128), f32),
            pltpu.VMEM((8, part, 128), f32),
            pltpu.VMEM((8, part, 128), f32),
            pltpu.VMEM((4, part, 128), f32),
            pltpu.VMEM((384, 128), f32),
            dma((8, 2)),
            dma((8, 2)),
            dma((2, 2 * PIECES, 4, 2)),
            dma((2,)),
            dma((8, 2)),
            dma((8, 2)),
            dma((4, 2)),
            dma((8, 2)),
            dma((2,)),
        ],
        compiler_params=pltpu.CompilerParams(
            collective_id=0, has_side_effects=True, vmem_limit_bytes=40 << 20
        ),
        name="gathered",
    )(precip, table, test, bins, thresholds)


def on_device(precip, thresholds, bin_index, test_matrix):
    days = precip.shape[0] * lax.axis_size("tm")
    points_total = precip.shape[1] * lax.axis_size(PTS)
    rows = harmonic_basis(days)
    table = np.zeros((lax.axis_size("tm"), ROWS, precip.shape[0]), np.float32)
    table[:, : len(rows)] = rows.reshape(len(rows), -1, precip.shape[0]).swapaxes(0, 1)
    sketch_t, blocks = gathered(
        precip, table, test_matrix, bin_index.reshape(-1, 128), thresholds, points_total
    )
    cross = jnp.concatenate(
        [
            jnp.concatenate([blocks[:128], blocks[128:256].T], 1),
            jnp.concatenate([blocks[128:256], blocks[256:]], 1),
        ],
        0,
    )
    lower = jnp.linalg.cholesky(cross)
    basis = lax.linalg.triangular_solve(
        lower, sketch_t, left_side=True, lower=True
    ).T
    return (basis, lower.T)


def solution(mesh):
    split = Mesh(mesh.devices.reshape(mesh.shape["tm"], 4, 8, 2), ("tm", *PTS))
    return jax.shard_map(
        on_device,
        mesh=split,
        in_specs=(P("tm", PTS), P(), P(PTS), P("tm", None)),
        out_specs=(P(PTS_TM, None), P()),
        check_vma=False,
    )
```

```python
import functools
import math

import jax
import jax.numpy as jnp
import numpy as np
from jax import lax
from jax.experimental import pallas as pl
from jax.experimental.pallas import tpu as pltpu
from jax.sharding import Mesh
from jax.sharding import PartitionSpec as P

HARM = 8
YEAR_DAYS = 365.25
ROWS = 24
PTS = ("pts_0", "pts_1", "pts_2")
PTS_TM = ("pts_0", "pts_1", "pts_2", "tm")
MESH = pl.DeviceIdType.MESH
HIGHEST = lax.Precision.HIGHEST


def harmonic_basis(days):
    day = np.arange(days, dtype=np.float32)
    columns = [np.ones(days)]
    for order in range(1, HARM + 1):
        phase = (np.float32(2.0 * math.pi * order / YEAR_DAYS) * day).astype(np.float64)
        columns += [np.cos(phase), np.sin(phase)]
    table = np.stack(columns)
    return np.linalg.solve(np.linalg.cholesky(table @ table.T), table)


def dot(a, b, dims):
    return lax.dot_general(
        a, b, (dims, ((), ())), precision=HIGHEST, preferred_element_type=jnp.float32
    )


def gather_kernel(
    scale,
    precip,
    table,
    test,
    bins,
    thresholds,
    sketch_out,
    cross_out,
    *scratch,
):
    (
        test_t,
        proj_out,
        proj_in,
        coef,
        level,
        sketch,
        ring,
        cross,
        core_in,
        y_in,
        z_in,
        x_in,
        total,
        proj_sem,
        coef_sem,
        ring_sem,
        core_sem,
        y_sem,
        z_sem,
        x_sem,
        gather_sem,
        join_sem,
    ) = scratch
    y = lax.axis_index("tm")
    x = lax.axis_index("pts_0")
    z = lax.axis_index("pts_1")
    c = lax.axis_index("pts_2")
    n_y, n_x, n_z = (lax.axis_size(a) for a in ("tm", "pts_0", "pts_1"))
    sends = []

    def send(src, dst, sem, device):
        copy = pltpu.make_async_remote_copy(
            src_ref=src,
            dst_ref=dst,
            send_sem=sem.at[0],
            recv_sem=sem.at[1],
            device_id=device,
            device_id_type=MESH,
        )
        copy.start()
        sends.append(copy)
        return copy

    y_at = lambda o: lax.rem(y + o + n_y, n_y)
    x_at = lambda o: lax.rem(x + o + n_x, n_x)
    z_at = lambda o: lax.rem(z + o + n_z, n_z)

    barrier = pltpu.get_barrier_semaphore()
    others = [{"tm": y_at(o)} for o in range(1, n_y)]
    others += [{"pts_0": x_at(o)} for o in range(1, n_x)]
    others += [{"pts_1": z_at(o)} for o in range(1, n_z)]
    others += [{"pts_2": 1 - c}]
    for other in others:
        pl.semaphore_signal(barrier, inc=1, device_id=other, device_id_type=MESH)

    mine = table[y]
    proj = dot(mine, precip[...], ((1,), (0,)))
    for r in range(n_y):
        proj_out[r] = proj[:, 128 * r : 128 * (r + 1)]
    pl.semaphore_wait(barrier, len(others))
    arrivals = []
    for o in [4, 3, 5, 2, 6, 1, 7]:
        arrivals.append(send(proj_out.at[y_at(o)], proj_in.at[o], proj_sem.at[o], {"tm": y_at(o)}))
    test_t[...] = test[...].T
    found = bins[...]
    value = jnp.zeros(found.shape, jnp.float32)
    for k in range(thresholds.shape[0]):
        value = jnp.where(found == k, thresholds[k], value)
    level[...] = value
    for copy in arrivals:
        copy.wait_recv()
    own = proj_out[y]
    for o in range(1, n_y):
        own = own + proj_in[o]
    coef[y] = own
    arrivals = []
    for o in [4, 3, 5, 2, 6, 1, 7]:
        arrivals.append(send(coef.at[y], coef.at[y], coef_sem.at[o], {"tm": y_at(o)}))
    for copy in arrivals:
        copy.wait_recv()

    def partial(o):
        r = y_at(o)
        fit = dot(mine, coef[r], ((0,), (0,)))
        data = precip[:, pl.ds(pl.multiple_of(128 * r, 128), 128)]
        excess = jnp.maximum(data - fit - level[pl.ds(r, 1), :], 0.0)
        sketch[o % n_y] = dot(test_t[...], excess, ((1,), (0,)))

    n_p = ring.shape[1] // 2
    piece = 128 // n_p

    def chain(way, q, step):
        hops = 4 if (q < n_p) == (way == 0) else 3
        if step > hops:
            return None
        o = hops + 1 - step
        return o if way == 0 else -o

    def rows_of(q):
        return pl.ds(q * piece, piece)

    def hop(way, q, step):
        o = chain(way, q, step) % n_y
        src = sketch.at[o, rows_of(q)] if step == 1 else ring.at[way, q, step - 2]
        return send(
            src,
            ring.at[way, q, step - 1],
            ring_sem.at[way, q, step - 1],
            {"tm": y_at(1 if way == 0 else -1)},
        )

    order = [(w, q) for q in range(n_p) for w in (0, 1)]
    long = [(w, q if w == 0 else q + n_p) for w, q in order]
    short = [(w, q + n_p if w == 0 else q) for w, q in order]
    moving = {}
    partial(4)
    for w, q in long:
        moving[w, q] = hop(w, q, 1)
    partial(3)
    for w, q in short:
        if w == 0:
            moving[w, q] = hop(w, q, 1)
    partial(-3)
    for w, q in short:
        if w == 1:
            moving[w, q] = hop(w, q, 1)
    partial(2)
    partial(-2)
    for step in (2, 3, 4):
        for w, q in long + short:
            o = chain(w, q, step)
            if o is None:
                continue
            moving[w, q].wait_recv()
            ring[w, q, step - 2] += sketch[o % n_y, rows_of(q)]
            moving[w, q] = hop(w, q, step)
        if step == 2:
            partial(1)
            partial(-1)
            partial(0)
    for q in range(2 * n_p):
        value = sketch[0, rows_of(q)]
        for w in (0, 1):
            hops = 4 if (w, q) in long else 3
            moving[w, q].wait_recv()
            value = value + ring[w, q, hops - 1]
        sketch_out[rows_of(q)] = value

    upper = sketch_out[:128]
    lower = sketch_out[128:]
    cross[:128] = dot(upper, upper, ((1,), (1,))) * scale
    cross[128:256] = dot(upper, lower, ((1,), (1,))) * scale
    cross[256:] = dot(lower, lower, ((1,), (1,))) * scale
    half = cross.shape[0] // 2
    part = half // n_y
    copy = send(
        cross.at[pl.ds(pl.multiple_of((1 - c) * half, 8), half)], core_in, core_sem, {"pts_2": 1 - c}
    )
    copy.wait_recv()
    core_in[...] += cross[pl.ds(pl.multiple_of(c * half, 8), half)]
    arrivals = []
    for o in [4, 3, 5, 2, 6, 1, 7]:
        arrivals.append(
            send(
                core_in.at[pl.ds(pl.multiple_of(y_at(o) * part, 8), part)],
                y_in.at[o],
                y_sem.at[o],
                {"tm": y_at(o)},
            )
        )
    for copy in arrivals:
        copy.wait_recv()
    own = core_in[pl.ds(pl.multiple_of(y * part, 8), part)]
    for o in range(1, n_y):
        own = own + y_in[o]
    z_in[z] = own
    arrivals = []
    for o in [4, 3, 5, 2, 6, 1, 7]:
        arrivals.append(send(z_in.at[z], z_in.at[z], z_sem.at[o], {"pts_1": z_at(o)}))
    for copy in arrivals:
        copy.wait_recv()
    own = z_in[0]
    for o in range(1, n_z):
        own = own + z_in[o]
    x_in[x] = own
    arrivals = []
    for o in [2, 1, 3]:
        arrivals.append(send(x_in.at[x], x_in.at[x], x_sem.at[o], {"pts_0": x_at(o)}))
    for copy in arrivals:
        copy.wait_recv()
    own = x_in[0]
    for o in range(1, n_x):
        own = own + x_in[o]
    place = pl.ds(pl.multiple_of(c * half + y * part, 8), part)
    total[place] = own
    arrivals = []
    for o in [4, 3, 5, 2, 6, 1, 7]:
        arrivals.append(send(total.at[place], total.at[place], gather_sem.at[o], {"tm": y_at(o)}))
    for copy in arrivals:
        copy.wait_recv()
    place = pl.ds(pl.multiple_of(c * half, 8), half)
    send(total.at[place], total.at[place], join_sem, {"pts_2": 1 - c}).wait_recv()
    cross_out[...] = total[...]
    for copy in sends:
        copy.wait_send()


PIECES = 2


def gathered(precip, table, test, bins, thresholds, points_total):
    vmem = pl.BlockSpec(memory_space=pltpu.VMEM)
    smem = pl.BlockSpec(memory_space=pltpu.SMEM)
    f32 = jnp.float32
    dma = pltpu.SemaphoreType.DMA
    half = 192
    part = 24
    return pl.pallas_call(
        functools.partial(gather_kernel, 1.0 / points_total),
        out_shape=(
            jax.ShapeDtypeStruct((256, 128), f32),
            jax.ShapeDtypeStruct((384, 128), f32),
        ),
        in_specs=[vmem, vmem, vmem, vmem, smem],
        out_specs=(vmem, vmem),
        scratch_shapes=[
            pltpu.VMEM((256, 256), f32),
            pltpu.VMEM((8, ROWS, 128), f32),
            pltpu.VMEM((8, ROWS, 128), f32),
            pltpu.VMEM((8, ROWS, 128), f32),
            pltpu.VMEM((8, 128), f32),
            pltpu.VMEM((8, 256, 128), f32),
            pltpu.VMEM((2, 2 * PIECES, 4, 128 // PIECES, 128), f32),
            pltpu.VMEM((384, 128), f32),
            pltpu.VMEM((half, 128), f32),
            pltpu.VMEM((8, part, 128), f32),
            pltpu.VMEM((8, part, 128), f32),
            pltpu.VMEM((4, part, 128), f32),
            pltpu.VMEM((384, 128), f32),
            dma((8, 2)),
            dma((8, 2)),
            dma((2, 2 * PIECES, 4, 2)),
            dma((2,)),
            dma((8, 2)),
            dma((8, 2)),
            dma((4, 2)),
            dma((8, 2)),
            dma((2,)),
        ],
        compiler_params=pltpu.CompilerParams(
            collective_id=0, has_side_effects=True, vmem_limit_bytes=40 << 20
        ),
        name="gathered",
    )(precip, table, test, bins, thresholds)


def terms(a):
    first = a.astype(jnp.bfloat16)
    rest = a - first.astype(jnp.float32)
    second = rest.astype(jnp.bfloat16)
    return first, second, (rest - second.astype(jnp.float32)).astype(jnp.bfloat16)


BLOCK = 32


def factor_kernel(cross, sketch, basis_out, factor_out, work):
    work[:128, :128] = cross[:128]
    work[:128, 128:256] = cross[128:256]
    work[128:, 128:256] = cross[256:]
    work[:, 256:] = sketch[...]
    factor_out[128:, :128] = jnp.zeros((128, 128), jnp.float32)
    sub = lax.broadcasted_iota(jnp.int32, (8, 128), 0)
    lane = lax.broadcasted_iota(jnp.int32, (8, 128), 1)
    wide = lambda row: jnp.broadcast_to(row, (8, 128))
    groups = BLOCK // 8
    for first in range(0, 256, BLOCK):
        tile, start = first // 128, first % 128
        tiles = range(tile, 3)
        rows = {
            (g, u): work[first + 8 * g : first + 8 * g + 8, 128 * u : 128 * u + 128]
            for g in range(groups)
            for u in tiles
        }
        done = {}
        for g in range(groups):
            at = start + 8 * g
            column = {
                (j, h): wide(rows[h, tile][:, at + j : at + j + 1])
                for j in range(8)
                for h in range(g, groups)
            }
            root = jnp.zeros((8, 128), jnp.float32)
            for j in range(8):
                pivot = wide(column[j, g][j : j + 1])
                inverse = 1.0 / pivot
                root = jnp.where(sub == j, lax.rsqrt(pivot), root)
                ratio = {h: column[j, h] * inverse for h in range(g, groups)}
                for k in range(j + 1, 8):
                    value = wide(column[j, g][k : k + 1])
                    for h in range(g, groups):
                        column[k, h] = column[k, h] - ratio[h] * value
                ratio[g] = jnp.where(sub > j, ratio[g], 0.0)
                for u in tiles:
                    row = wide(rows[g, u][j : j + 1])
                    for h in range(g if j < 7 else g + 1, groups):
                        rows[h, u] = rows[h, u] - ratio[h] * row
            place = slice(first + 8 * g, first + 8 * g + 8)
            for u in tiles:
                value = rows[g, u] * root
                if u == tile:
                    value = jnp.where(lane >= at + sub, value, 0.0)
                done[g, u] = value
                if u < 2:
                    factor_out[place, 128 * u : 128 * u + 128] = value
                else:
                    work[place, 256:] = value
        after = first + BLOCK
        if after >= 256:
            break
        base = 128 * tile
        panel = jnp.concatenate(
            [jnp.concatenate([done[g, u] for u in tiles], 1) for g in range(groups)], 0
        )
        one, two, three = terms(panel)
        left = jnp.concatenate([one, one, two, two, one, three], 0)[:, : 256 - base].T
        right = jnp.concatenate([one, two, one, two, three, one], 0)
        ends = sorted({after, after + BLOCK, max(after, 128), 256})
        for low, high in zip(ends, ends[1:]):
            edge = 128 * (low // 128)
            work[low:high, edge:] -= jnp.dot(
                left[low - base : high - base],
                right[:, edge - base :],
                preferred_element_type=jnp.float32,
            )
    basis_out[:, :128] = work[:128, 256:].T
    basis_out[:, 128:] = work[128:, 256:].T


def factored(cross, sketch):
    vmem = pl.BlockSpec(memory_space=pltpu.VMEM)
    f32 = jnp.float32
    return pl.pallas_call(
        factor_kernel,
        out_shape=(
            jax.ShapeDtypeStruct((128, 256), f32),
            jax.ShapeDtypeStruct((256, 256), f32),
        ),
        in_specs=[vmem, vmem],
        out_specs=(vmem, vmem),
        scratch_shapes=[pltpu.VMEM((256, 384), f32)],
        compiler_params=pltpu.CompilerParams(vmem_limit_bytes=40 << 20),
        name="factored",
    )(cross, sketch)


def on_device(precip, thresholds, bin_index, test_matrix):
    days = precip.shape[0] * lax.axis_size("tm")
    points_total = precip.shape[1] * lax.axis_size(PTS)
    rows = harmonic_basis(days)
    table = np.zeros((lax.axis_size("tm"), ROWS, precip.shape[0]), np.float32)
    table[:, : len(rows)] = rows.reshape(len(rows), -1, precip.shape[0]).swapaxes(0, 1)
    sketch_t, blocks = gathered(
        precip, table, test_matrix, bin_index.reshape(-1, 128), thresholds, points_total
    )
    return factored(blocks, sketch_t)


def solution(mesh):
    split = Mesh(mesh.devices.reshape(mesh.shape["tm"], 4, 8, 2), ("tm", *PTS))
    return jax.shard_map(
        on_device,
        mesh=split,
        in_specs=(P("tm", PTS), P(), P(PTS), P("tm", None)),
        out_specs=(P(PTS_TM, None), P()),
        check_vma=False,
    )
```

```python
import functools
import math

import jax
import jax.numpy as jnp
import numpy as np
from jax import lax
from jax.experimental import pallas as pl
from jax.experimental.pallas import tpu as pltpu
from jax.sharding import Mesh
from jax.sharding import PartitionSpec as P

HARM = 8
YEAR_DAYS = 365.25
ROWS = 24
PTS = ("pts_0", "pts_1", "pts_2")
PTS_TM = ("pts_0", "pts_1", "pts_2", "tm")
MESH = pl.DeviceIdType.MESH
HIGHEST = lax.Precision.HIGHEST


def harmonic_basis(days):
    day = np.arange(days, dtype=np.float32)
    columns = [np.ones(days)]
    for order in range(1, HARM + 1):
        phase = (np.float32(2.0 * math.pi * order / YEAR_DAYS) * day).astype(np.float64)
        columns += [np.cos(phase), np.sin(phase)]
    table = np.stack(columns)
    return np.linalg.solve(np.linalg.cholesky(table @ table.T), table)


def dot(a, b, dims):
    return lax.dot_general(
        a, b, (dims, ((), ())), precision=HIGHEST, preferred_element_type=jnp.float32
    )


def gather_kernel(
    scale,
    precip_hbm,
    table_hbm,
    test_hbm,
    bins_hbm,
    thresholds_hbm,
    sketch_out,
    cross_out,
    *scratch,
):
    (
        precip,
        table,
        test,
        bins,
        thresholds,
        load_sem,
        test_t,
        proj_out,
        proj_in,
        coef,
        level,
        sketch,
        ring,
        cross,
        core_in,
        y_in,
        z_in,
        x_in,
        total,
        proj_sem,
        coef_sem,
        ring_sem,
        core_sem,
        y_sem,
        z_sem,
        x_sem,
        gather_sem,
        join_sem,
    ) = scratch
    y = lax.axis_index("tm")
    x = lax.axis_index("pts_0")
    z = lax.axis_index("pts_1")
    c = lax.axis_index("pts_2")
    n_y, n_x, n_z = (lax.axis_size(a) for a in ("tm", "pts_0", "pts_1"))
    sends = []


    def send(src, dst, sem, device):
        copy = pltpu.make_async_remote_copy(
            src_ref=src,
            dst_ref=dst,
            send_sem=sem.at[0],
            recv_sem=sem.at[1],
            device_id=device,
            device_id_type=MESH,
        )
        copy.start()
        sends.append(copy)
        return copy

    y_at = lambda o: lax.rem(y + o + n_y, n_y)
    x_at = lambda o: lax.rem(x + o + n_x, n_x)
    z_at = lambda o: lax.rem(z + o + n_z, n_z)

    barrier = pltpu.get_barrier_semaphore()
    others = [{"tm": y_at(o)} for o in range(1, n_y)]
    others += [{"pts_0": x_at(o)} for o in range(1, n_x)]
    others += [{"pts_1": z_at(o)} for o in range(1, n_z)]
    others += [{"pts_2": 1 - c}]
    for other in others:
        pl.semaphore_signal(barrier, inc=1, device_id=other, device_id_type=MESH)

    loads = [
        pltpu.make_async_copy(src, dst, load_sem.at[i])
        for i, (src, dst) in enumerate(
            [
                (table_hbm.at[y], table),
                (precip_hbm, precip),
                (test_hbm, test),
                (bins_hbm, bins),
                (thresholds_hbm, thresholds),
            ]
        )
    ]
    for copy in loads:
        copy.start()

    loads[0].wait()
    loads[1].wait()
    mine = table[...]
    proj = dot(mine, precip[...], ((1,), (0,)))
    for r in range(n_y):
        proj_out[r] = proj[:, 128 * r : 128 * (r + 1)]
    pl.semaphore_wait(barrier, len(others))
    arrivals = []
    for o in [4, 3, 5, 2, 6, 1, 7]:
        arrivals.append(send(proj_out.at[y_at(o)], proj_in.at[o], proj_sem.at[o], {"tm": y_at(o)}))
    for copy in loads[2:]:
        copy.wait()
    test_t[...] = test[...].T
    found = bins[...]
    value = jnp.zeros(found.shape, jnp.float32)
    for k in range(thresholds.shape[0]):
        value = jnp.where(found == k, thresholds[k], value)
    level[...] = value
    for copy in arrivals:
        copy.wait_recv()
    own = proj_out[y]
    for o in range(1, n_y):
        own = own + proj_in[o]
    coef[y] = own
    arrivals = []
    for o in [4, 3, 5, 2, 6, 1, 7]:
        arrivals.append(send(coef.at[y], coef.at[y], coef_sem.at[o], {"tm": y_at(o)}))
    for copy in arrivals:
        copy.wait_recv()

    def partial(o):
        r = y_at(o)
        fit = dot(mine, coef[r], ((0,), (0,)))
        data = precip[:, pl.ds(pl.multiple_of(128 * r, 128), 128)]
        excess = jnp.maximum(data - fit - level[pl.ds(r, 1), :], 0.0)
        sketch[o % n_y] = dot(test_t[...], excess, ((1,), (0,)))

    n_p = ring.shape[1] // 2
    piece = 128 // n_p

    def chain(way, q, step):
        hops = 4 if (q < n_p) == (way == 0) else 3
        if step > hops:
            return None
        o = hops + 1 - step
        return o if way == 0 else -o

    def rows_of(q):
        return pl.ds(q * piece, piece)

    def hop(way, q, step):
        o = chain(way, q, step) % n_y
        src = sketch.at[o, rows_of(q)] if step == 1 else ring.at[way, q, step - 2]
        return send(
            src,
            ring.at[way, q, step - 1],
            ring_sem.at[way, q, step - 1],
            {"tm": y_at(1 if way == 0 else -1)},
        )

    order = [(w, q) for q in range(n_p) for w in (0, 1)]
    long = [(w, q if w == 0 else q + n_p) for w, q in order]
    short = [(w, q + n_p if w == 0 else q) for w, q in order]
    moving = {}
    partial(4)
    for w, q in long:
        moving[w, q] = hop(w, q, 1)
    partial(3)
    for w, q in short:
        if w == 0:
            moving[w, q] = hop(w, q, 1)
    partial(-3)
    for w, q in short:
        if w == 1:
            moving[w, q] = hop(w, q, 1)
    partial(2)
    partial(-2)
    for step in (2, 3, 4):
        for w, q in long + short:
            o = chain(w, q, step)
            if o is None:
                continue
            moving[w, q].wait_recv()
            ring[w, q, step - 2] += sketch[o % n_y, rows_of(q)]
            moving[w, q] = hop(w, q, step)
        if step == 2:
            partial(1)
            partial(-1)
            partial(0)
    for q in range(2 * n_p):
        value = sketch[0, rows_of(q)]
        for w in (0, 1):
            hops = 4 if (w, q) in long else 3
            moving[w, q].wait_recv()
            value = value + ring[w, q, hops - 1]
        sketch_out[rows_of(q)] = value

    upper = sketch_out[:128]
    lower = sketch_out[128:]
    cross[:128] = dot(upper, upper, ((1,), (1,))) * scale
    cross[128:256] = dot(upper, lower, ((1,), (1,))) * scale
    cross[256:] = dot(lower, lower, ((1,), (1,))) * scale
    half = cross.shape[0] // 2
    part = half // n_y
    copy = send(
        cross.at[pl.ds(pl.multiple_of((1 - c) * half, 8), half)], core_in, core_sem, {"pts_2": 1 - c}
    )
    copy.wait_recv()
    core_in[...] += cross[pl.ds(pl.multiple_of(c * half, 8), half)]
    arrivals = []
    for o in [4, 3, 5, 2, 6, 1, 7]:
        arrivals.append(
            send(
                core_in.at[pl.ds(pl.multiple_of(y_at(o) * part, 8), part)],
                y_in.at[o],
                y_sem.at[o],
                {"tm": y_at(o)},
            )
        )
    for copy in arrivals:
        copy.wait_recv()
    own = core_in[pl.ds(pl.multiple_of(y * part, 8), part)]
    for o in range(1, n_y):
        own = own + y_in[o]
    z_in[z] = own
    arrivals = []
    for o in [4, 3, 5, 2, 6, 1, 7]:
        arrivals.append(send(z_in.at[z], z_in.at[z], z_sem.at[o], {"pts_1": z_at(o)}))
    for copy in arrivals:
        copy.wait_recv()
    own = z_in[0]
    for o in range(1, n_z):
        own = own + z_in[o]
    x_in[x] = own
    arrivals = []
    for o in [2, 1, 3]:
        arrivals.append(send(x_in.at[x], x_in.at[x], x_sem.at[o], {"pts_0": x_at(o)}))
    for copy in arrivals:
        copy.wait_recv()
    own = x_in[0]
    for o in range(1, n_x):
        own = own + x_in[o]
    place = pl.ds(pl.multiple_of(c * half + y * part, 8), part)
    total[place] = own
    arrivals = []
    for o in [4, 3, 5, 2, 6, 1, 7]:
        arrivals.append(send(total.at[place], total.at[place], gather_sem.at[o], {"tm": y_at(o)}))
    for copy in arrivals:
        copy.wait_recv()
    place = pl.ds(pl.multiple_of(c * half, 8), half)
    send(total.at[place], total.at[place], join_sem, {"pts_2": 1 - c}).wait_recv()
    cross_out[...] = total[...]
    for copy in sends:
        copy.wait_send()


PIECES = 2


def gathered(precip, table, test, bins, thresholds, points_total):
    vmem = pl.BlockSpec(memory_space=pltpu.VMEM)
    hbm = pl.BlockSpec(memory_space=pltpu.HBM)
    f32 = jnp.float32
    dma = pltpu.SemaphoreType.DMA
    half = 192
    part = 24
    operands = (precip, table, test, bins, thresholds)
    return pl.pallas_call(
        functools.partial(gather_kernel, 1.0 / points_total),
        out_shape=(
            jax.ShapeDtypeStruct((256, 128), f32),
            jax.ShapeDtypeStruct((384, 128), f32),
        ),
        in_specs=[hbm] * 5,
        out_specs=(vmem, vmem),
        scratch_shapes=[
            pltpu.VMEM(precip.shape, f32),
            pltpu.VMEM(table.shape[1:], f32),
            pltpu.VMEM(test.shape, f32),
            pltpu.VMEM(bins.shape, jnp.int32),
            pltpu.SMEM(thresholds.shape, f32),
            dma((5,)),
            pltpu.VMEM((256, 256), f32),
            pltpu.VMEM((8, ROWS, 128), f32),
            pltpu.VMEM((8, ROWS, 128), f32),
            pltpu.VMEM((8, ROWS, 128), f32),
            pltpu.VMEM((8, 128), f32),
            pltpu.VMEM((8, 256, 128), f32),
            pltpu.VMEM((2, 2 * PIECES, 4, 128 // PIECES, 128), f32),
            pltpu.VMEM((384, 128), f32),
            pltpu.VMEM((half, 128), f32),
            pltpu.VMEM((8, part, 128), f32),
            pltpu.VMEM((8, part, 128), f32),
            pltpu.VMEM((4, part, 128), f32),
            pltpu.VMEM((384, 128), f32),
            dma((8, 2)),
            dma((8, 2)),
            dma((2, 2 * PIECES, 4, 2)),
            dma((2,)),
            dma((8, 2)),
            dma((8, 2)),
            dma((4, 2)),
            dma((8, 2)),
            dma((2,)),
        ],
        compiler_params=pltpu.CompilerParams(
            collective_id=0, has_side_effects=True, vmem_limit_bytes=40 << 20
        ),
        name="gathered",
    )(*(pltpu.with_memory_space_constraint(a, pltpu.HBM) for a in operands))


def terms(a):
    first = a.astype(jnp.bfloat16)
    rest = a - first.astype(jnp.float32)
    second = rest.astype(jnp.bfloat16)
    return first, second, (rest - second.astype(jnp.float32)).astype(jnp.bfloat16)


BLOCK = 32


def factor_kernel(cross, sketch, basis_out, factor_out, work):
    work[:128, :128] = cross[:128]
    work[:128, 128:256] = cross[128:256]
    work[128:, 128:256] = cross[256:]
    work[:, 256:] = sketch[...]
    factor_out[128:, :128] = jnp.zeros((128, 128), jnp.float32)
    sub = lax.broadcasted_iota(jnp.int32, (8, 128), 0)
    lane = lax.broadcasted_iota(jnp.int32, (8, 128), 1)
    wide = lambda row: jnp.broadcast_to(row, (8, 128))
    groups = BLOCK // 8
    for first in range(0, 256, BLOCK):
        tile, start = first // 128, first % 128
        tiles = range(tile, 3)
        rows = {
            (g, u): work[first + 8 * g : first + 8 * g + 8, 128 * u : 128 * u + 128]
            for g in range(groups)
            for u in tiles
        }
        done = {}
        for g in range(groups):
            at = start + 8 * g
            column = {
                (j, h): wide(rows[h, tile][:, at + j : at + j + 1])
                for j in range(8)
                for h in range(g, groups)
            }
            root = jnp.zeros((8, 128), jnp.float32)
            for j in range(8):
                pivot = wide(column[j, g][j : j + 1])
                inverse = 1.0 / pivot
                root = jnp.where(sub == j, lax.rsqrt(pivot), root)
                ratio = {h: column[j, h] * inverse for h in range(g, groups)}
                for k in range(j + 1, 8):
                    value = wide(column[j, g][k : k + 1])
                    for h in range(g, groups):
                        column[k, h] = column[k, h] - ratio[h] * value
                ratio[g] = jnp.where(sub > j, ratio[g], 0.0)
                for u in tiles:
                    row = wide(rows[g, u][j : j + 1])
                    for h in range(g if j < 7 else g + 1, groups):
                        rows[h, u] = rows[h, u] - ratio[h] * row
            place = slice(first + 8 * g, first + 8 * g + 8)
            for u in tiles:
                value = rows[g, u] * root
                if u == tile:
                    value = jnp.where(lane >= at + sub, value, 0.0)
                done[g, u] = value
                if u < 2:
                    factor_out[place, 128 * u : 128 * u + 128] = value
                else:
                    work[place, 256:] = value
        after = first + BLOCK
        if after >= 256:
            break
        base = 128 * tile
        panel = jnp.concatenate(
            [jnp.concatenate([done[g, u] for u in tiles], 1) for g in range(groups)], 0
        )
        one, two, three = terms(panel)
        left = jnp.concatenate([one, one, two, two, one, three], 0)[:, : 256 - base].T
        right = jnp.concatenate([one, two, one, two, three, one], 0)
        ends = sorted({after, after + BLOCK, max(after, 128), 256})
        for low, high in zip(ends, ends[1:]):
            edge = 128 * (low // 128)
            work[low:high, edge:] -= jnp.dot(
                left[low - base : high - base],
                right[:, edge - base :],
                preferred_element_type=jnp.float32,
            )
    basis_out[:, :128] = work[:128, 256:].T
    basis_out[:, 128:] = work[128:, 256:].T


def factored(cross, sketch):
    vmem = pl.BlockSpec(memory_space=pltpu.VMEM)
    f32 = jnp.float32
    return pl.pallas_call(
        factor_kernel,
        out_shape=(
            jax.ShapeDtypeStruct((128, 256), f32),
            jax.ShapeDtypeStruct((256, 256), f32),
        ),
        in_specs=[vmem, vmem],
        out_specs=(vmem, vmem),
        scratch_shapes=[pltpu.VMEM((256, 384), f32)],
        compiler_params=pltpu.CompilerParams(vmem_limit_bytes=40 << 20),
        name="factored",
    )(cross, sketch)


def on_device(precip, thresholds, bin_index, test_matrix):
    days = precip.shape[0] * lax.axis_size("tm")
    points_total = precip.shape[1] * lax.axis_size(PTS)
    rows = harmonic_basis(days)
    table = np.zeros((lax.axis_size("tm"), ROWS, precip.shape[0]), np.float32)
    table[:, : len(rows)] = rows.reshape(len(rows), -1, precip.shape[0]).swapaxes(0, 1)
    sketch_t, blocks = gathered(
        precip, table, test_matrix, bin_index.reshape(-1, 128), thresholds, points_total
    )
    return factored(blocks, sketch_t)


def solution(mesh):
    split = Mesh(mesh.devices.reshape(mesh.shape["tm"], 4, 8, 2), ("tm", *PTS))
    return jax.shard_map(
        on_device,
        mesh=split,
        in_specs=(P("tm", PTS), P(), P(PTS), P("tm", None)),
        out_specs=(P(PTS_TM, None), P()),
        check_vma=False,
    )
```

```python
import functools
import math

import jax
import jax.numpy as jnp
import numpy as np
from jax import lax
from jax.experimental import pallas as pl
from jax.experimental.pallas import tpu as pltpu
from jax.sharding import Mesh
from jax.sharding import PartitionSpec as P

HARM = 8
YEAR_DAYS = 365.25
ROWS = 24
PTS = ("pts_0", "pts_1", "pts_2")
PTS_TM = ("pts_0", "pts_1", "pts_2", "tm")
MESH = pl.DeviceIdType.MESH


def harmonic_basis(days):
    day = np.arange(days, dtype=np.float32)
    columns = [np.ones(days)]
    for order in range(1, HARM + 1):
        phase = (np.float32(2.0 * math.pi * order / YEAR_DAYS) * day).astype(np.float64)
        columns += [np.cos(phase), np.sin(phase)]
    table = np.stack(columns)
    return np.linalg.solve(np.linalg.cholesky(table @ table.T), table)


def terms(a):
    first = a.astype(jnp.bfloat16)
    rest = a - first.astype(jnp.float32)
    second = rest.astype(jnp.bfloat16)
    return first, second, (rest - second.astype(jnp.float32)).astype(jnp.bfloat16)


LEFT, RIGHT = (0, 0, 1, 1, 0, 2), (0, 1, 0, 1, 2, 0)


def left_of(parts, dim, count=6):
    return jnp.concatenate([parts[i] for i in LEFT[:count]], dim)


def right_of(parts, dim, count=6):
    return jnp.concatenate([parts[i] for i in RIGHT[:count]], dim)


def dot(a, b, dims=((1,), (0,))):
    return lax.dot_general(a, b, (dims, ((), ())), preferred_element_type=jnp.float32)


def gather_kernel(
    scale,
    precip_hbm,
    table_hbm,
    test_hbm,
    bins_hbm,
    thresholds_hbm,
    sketch_out,
    cross_out,
    *scratch,
):
    (
        precip,
        table,
        test,
        bins,
        thresholds,
        load_sem,
        test_t,
        table_t,
        proj_out,
        proj_in,
        coef,
        level,
        sketch,
        ring,
        cross,
        core_in,
        y_in,
        z_in,
        x_in,
        total,
        proj_sem,
        coef_sem,
        ring_sem,
        core_sem,
        y_sem,
        z_sem,
        x_sem,
        gather_sem,
        join_sem,
    ) = scratch
    y = lax.axis_index("tm")
    x = lax.axis_index("pts_0")
    z = lax.axis_index("pts_1")
    c = lax.axis_index("pts_2")
    n_y, n_x, n_z = (lax.axis_size(a) for a in ("tm", "pts_0", "pts_1"))
    sends = []


    def send(src, dst, sem, device):
        copy = pltpu.make_async_remote_copy(
            src_ref=src,
            dst_ref=dst,
            send_sem=sem.at[0],
            recv_sem=sem.at[1],
            device_id=device,
            device_id_type=MESH,
        )
        copy.start()
        sends.append(copy)
        return copy

    y_at = lambda o: lax.rem(y + o + n_y, n_y)
    x_at = lambda o: lax.rem(x + o + n_x, n_x)
    z_at = lambda o: lax.rem(z + o + n_z, n_z)

    barrier = pltpu.get_barrier_semaphore()
    others = [{"tm": y_at(o)} for o in range(1, n_y)]
    others += [{"pts_0": x_at(o)} for o in range(1, n_x)]
    others += [{"pts_1": z_at(o)} for o in range(1, n_z)]
    others += [{"pts_2": 1 - c}]
    for other in others:
        pl.semaphore_signal(barrier, inc=1, device_id=other, device_id_type=MESH)

    loads = [
        pltpu.make_async_copy(src, dst, load_sem.at[i])
        for i, (src, dst) in enumerate(
            [
                (table_hbm.at[y], table),
                (precip_hbm, precip),
                (test_hbm, test),
                (bins_hbm, bins),
                (thresholds_hbm, thresholds),
            ]
        )
    ]
    for copy in loads:
        copy.start()

    loads[0].wait()
    loads[1].wait()
    one, two, three = terms(table[...])
    stack = jnp.concatenate([one, two, three], 0)
    for r in range(0, n_y, 2):
        data = terms(precip[:, 128 * r : 128 * (r + 2)])
        proj = dot(stack, data[0])
        more = dot(stack[:64], data[1])
        proj = proj[:32] + proj[32:64] + proj[64:] + more[:32] + more[32:] + dot(stack[:32], data[2])
        proj_out[r] = proj[:ROWS, :128]
        proj_out[r + 1] = proj[:ROWS, 128:]
    pl.semaphore_wait(barrier, len(others))
    arrivals = []
    for o in [4, 3, 5, 2, 6, 1, 7]:
        arrivals.append(send(proj_out.at[y_at(o)], proj_in.at[o], proj_sem.at[o], {"tm": y_at(o)}))
    for copy in loads[2:]:
        copy.wait()
    test_t[...] = left_of(terms(test[...].T), 1, TERMS)
    table_t[...] = left_of((one, two, three), 0).T
    found = bins[...]
    value = jnp.zeros(found.shape, jnp.float32)
    for k in range(thresholds.shape[0]):
        value = jnp.where(found == k, thresholds[k], value)
    level[...] = value
    for copy in arrivals:
        copy.wait_recv()
    own = proj_out[y]
    for o in range(1, n_y):
        own = own + proj_in[o]
    coef[y] = own
    arrivals = []
    for o in [4, 3, 5, 2, 6, 1, 7]:
        arrivals.append(send(coef.at[y], coef.at[y], coef_sem.at[o], {"tm": y_at(o)}))
    for copy in arrivals:
        copy.wait_recv()

    def partial(pair):
        join = lambda f: jnp.concatenate([f(y_at(o)) for o in pair], 1)
        found = join(lambda r: coef[r])
        found = jnp.concatenate([found, jnp.zeros((32 - ROWS, found.shape[1]), jnp.float32)], 0)
        fit = dot(table_t[...], right_of(terms(found), 0))
        data = join(lambda r: precip[:, pl.ds(pl.multiple_of(128 * r, 128), 128)])
        excess = jnp.maximum(data - fit - join(lambda r: level[pl.ds(r, 1), :]), 0.0)
        sums = dot(test_t[...], right_of(terms(excess), 0, TERMS))
        for i, o in enumerate(pair):
            sketch[o % n_y] = sums[:, 128 * i : 128 * i + 128]

    edges = [(h, s * a * t, s * b * t) for h, s in ((0, 1), (1, -1)) for side, t in ((LONG, -1), (SHORT, 1)) for a, b in side]
    level_of = lambda e: max((1 + level_of(f) for f in edges if f[0] == e[0] and f[2] == e[1]), default=0)
    edges.sort(key=lambda e: (level_of(e), -abs(e[1])))
    piece = 128 // PIECES
    moving = {}
    ready = set()

    def need(o):
        for pair in PAIRS:
            if o in [p % n_y for p in pair] and pair not in ready:
                partial(pair)
                ready.add(pair)

    def arrived(h, a, q):
        rows = pl.ds(128 * h + q * piece, piece)
        value = sketch[-a % n_y, rows]
        for i, e in enumerate(edges):
            if e[0] == h and e[2] == a:
                moving[i, q].wait_recv()
                value = value + ring[i, pl.ds(q * piece, piece)]
        return value

    for i, (h, a, b) in enumerate(edges):
        inner = [j for j, e in enumerate(edges) if e[0] == h and e[2] == a]
        need(-a % n_y)
        for q in range(PIECES):
            if inner:
                src = ring.at[inner[0], pl.ds(q * piece, piece)]
                src[...] = arrived(h, a, q)
            else:
                src = sketch.at[-a % n_y, pl.ds(128 * h + q * piece, piece)]
            moving[i, q] = send(
                src, ring.at[i, pl.ds(q * piece, piece)], ring_sem.at[i, q], {"tm": y_at(b - a)}
            )
        if i == EARLY:
            for o in range(n_y):
                need(o)
    for h in (0, 1):
        for q in range(PIECES):
            sketch_out[pl.ds(128 * h + q * piece, piece)] = arrived(h, 0, q)

    parts = terms(sketch_out[...])
    left = left_of(parts, 1)
    right = right_of(parts, 1)
    cross[:128] = dot(left[:128], right[:128], ((1,), (1,))) * scale
    cross[128:256] = dot(left[:128], right[128:], ((1,), (1,))) * scale
    cross[256:] = dot(left[128:], right[128:], ((1,), (1,))) * scale
    half = cross.shape[0] // 2
    part = half // n_y
    copy = send(
        cross.at[pl.ds(pl.multiple_of((1 - c) * half, 8), half)], core_in, core_sem, {"pts_2": 1 - c}
    )
    copy.wait_recv()
    core_in[...] += cross[pl.ds(pl.multiple_of(c * half, 8), half)]
    arrivals = []
    for o in [4, 3, 5, 2, 6, 1, 7]:
        arrivals.append(
            send(
                core_in.at[pl.ds(pl.multiple_of(y_at(o) * part, 8), part)],
                y_in.at[o],
                y_sem.at[o],
                {"tm": y_at(o)},
            )
        )
    for copy in arrivals:
        copy.wait_recv()
    own = core_in[pl.ds(pl.multiple_of(y * part, 8), part)]
    for o in range(1, n_y):
        own = own + y_in[o]
    z_in[z] = own
    arrivals = []
    for o in [4, 3, 5, 2, 6, 1, 7]:
        arrivals.append(send(z_in.at[z], z_in.at[z], z_sem.at[o], {"pts_1": z_at(o)}))
    for copy in arrivals:
        copy.wait_recv()
    own = z_in[0]
    for o in range(1, n_z):
        own = own + z_in[o]
    x_in[x] = own
    arrivals = []
    for o in [2, 1, 3]:
        arrivals.append(send(x_in.at[x], x_in.at[x], x_sem.at[o], {"pts_0": x_at(o)}))
    for copy in arrivals:
        copy.wait_recv()
    own = x_in[0]
    for o in range(1, n_x):
        own = own + x_in[o]
    place = pl.ds(pl.multiple_of(c * half + y * part, 8), part)
    total[place] = own
    arrivals = []
    for o in [4, 3, 5, 2, 6, 1, 7]:
        arrivals.append(send(total.at[place], total.at[place], gather_sem.at[o], {"tm": y_at(o)}))
    for copy in arrivals:
        copy.wait_recv()
    place = pl.ds(pl.multiple_of(c * half, 8), half)
    send(total.at[place], total.at[place], join_sem, {"pts_2": 1 - c}).wait_recv()
    cross_out[...] = total[...]
    for copy in sends:
        copy.wait_send()


PIECES = 2
TERMS = 3
PAIRS = ((4, 3), (-3, 2), (-2, 1), (-1, 0))
EARLY = 5
LONG = ((4, 2), (3, 2), (2, 1), (1, 0))
SHORT = ((3, 2), (2, 1), (1, 0))


def gathered(precip, table, test, bins, thresholds, points_total):
    vmem = pl.BlockSpec(memory_space=pltpu.VMEM)
    hbm = pl.BlockSpec(memory_space=pltpu.HBM)
    f32 = jnp.float32
    dma = pltpu.SemaphoreType.DMA
    half = 192
    part = 24
    operands = (precip, table, test, bins, thresholds)
    return pl.pallas_call(
        functools.partial(gather_kernel, 1.0 / points_total),
        out_shape=(
            jax.ShapeDtypeStruct((256, 128), f32),
            jax.ShapeDtypeStruct((384, 128), f32),
        ),
        in_specs=[hbm] * 5,
        out_specs=(vmem, vmem),
        scratch_shapes=[
            pltpu.VMEM(precip.shape, f32),
            pltpu.VMEM(table.shape[1:], f32),
            pltpu.VMEM(test.shape, f32),
            pltpu.VMEM(bins.shape, jnp.int32),
            pltpu.SMEM(thresholds.shape, f32),
            dma((5,)),
            pltpu.VMEM((256, 256 * TERMS), jnp.bfloat16),
            pltpu.VMEM((256, 192), jnp.bfloat16),
            pltpu.VMEM((8, ROWS, 128), f32),
            pltpu.VMEM((8, ROWS, 128), f32),
            pltpu.VMEM((8, ROWS, 128), f32),
            pltpu.VMEM((8, 128), f32),
            pltpu.VMEM((8, 256, 128), f32),
            pltpu.VMEM((14, 128, 128), f32),
            pltpu.VMEM((384, 128), f32),
            pltpu.VMEM((half, 128), f32),
            pltpu.VMEM((8, part, 128), f32),
            pltpu.VMEM((8, part, 128), f32),
            pltpu.VMEM((4, part, 128), f32),
            pltpu.VMEM((384, 128), f32),
            dma((8, 2)),
            dma((8, 2)),
            dma((14, PIECES, 2)),
            dma((2,)),
            dma((8, 2)),
            dma((8, 2)),
            dma((4, 2)),
            dma((8, 2)),
            dma((2,)),
        ],
        compiler_params=pltpu.CompilerParams(
            collective_id=0, has_side_effects=True, vmem_limit_bytes=40 << 20
        ),
        name="gathered",
    )(*(pltpu.with_memory_space_constraint(a, pltpu.HBM) for a in operands))


BLOCK = 32
STRIP = 16


def factor_kernel(cross, sketch, basis_out, factor_out, work):
    factor_out[128:, :128] = jnp.zeros((128, 128), jnp.float32)
    sub = lax.broadcasted_iota(jnp.int32, (8, 128), 0)
    lane = lax.broadcasted_iota(jnp.int32, (8, 128), 1)
    wide = lambda row: jnp.broadcast_to(row, (8, 128))
    groups = BLOCK // 8

    def source(low, high, u):
        if u == 2:
            return sketch[low:high]
        return cross[128 * u + low : 128 * u + high] if low < 128 else cross[128 + low : 128 + high]

    for first in range(0, 256, BLOCK):
        tile, start = first // 128, first % 128
        tiles = range(tile, 3)
        rows = {}
        for g in range(groups):
            low = first + 8 * g
            for u in tiles:
                rows[g, u] = (
                    work[low : low + 8, 128 * u : 128 * u + 128] if first else source(low, low + 8, u)
                )
        root = {g: jnp.zeros((8, 128), jnp.float32) for g in range(groups)}
        for open_at in range(0, BLOCK, STRIP):
            strip = range(open_at, open_at + STRIP)
            column = {
                (j, h): wide(rows[h, tile][:, start + j : start + j + 1])
                for j in strip
                for h in range(j // 8, groups)
            }
            for j in strip:
                g, i = divmod(j, 8)
                pivot = wide(column[j, g][i : i + 1])
                inverse = 1.0 / pivot
                root[g] = jnp.where(sub == i, lax.rsqrt(pivot), root[g])
                ratio = {h: column[j, h] * inverse for h in range(g, groups)}
                for k in range(j + 1, strip.stop):
                    value = wide(column[j, k // 8][k % 8 : k % 8 + 1])
                    for h in range(k // 8, groups):
                        column[k, h] = column[k, h] - ratio[h] * value
                ratio[g] = jnp.where(sub > i, ratio[g], 0.0)
                for u in tiles:
                    row = wide(rows[g, u][i : i + 1])
                    for h in range(g if i < 7 else g + 1, groups):
                        rows[h, u] = rows[h, u] - ratio[h] * row
        done = {}
        for g in range(groups):
            place = slice(first + 8 * g, first + 8 * g + 8)
            for u in tiles:
                value = rows[g, u] * root[g]
                if u == tile:
                    value = jnp.where(lane >= start + 8 * g + sub, value, 0.0)
                done[g, u] = value
                if u < 2:
                    factor_out[place, 128 * u : 128 * u + 128] = value
                else:
                    work[place, 256:] = value
        after = first + BLOCK
        if after >= 256:
            break
        base = 128 * tile
        panel = jnp.concatenate(
            [jnp.concatenate([done[g, u] for u in tiles], 1) for g in range(groups)], 0
        )
        parts = terms(panel)
        left = left_of(parts, 0)[:, : 256 - base].T
        right = right_of(parts, 0)
        ends = sorted({after, after + BLOCK, max(after, 128), 256})
        for low, high in zip(ends, ends[1:]):
            edge = 128 * (low // 128)
            change = dot(left[low - base : high - base], right[:, edge - base :])
            for u in range(edge // 128, 3):
                old = work[low:high, 128 * u : 128 * u + 128] if first else source(low, high, u)
                at = 128 * u - edge
                work[low:high, 128 * u : 128 * u + 128] = old - change[:, at : at + 128]
    basis_out[:, :128] = work[:128, 256:].T
    basis_out[:, 128:] = work[128:, 256:].T


def factored(cross, sketch):
    vmem = pl.BlockSpec(memory_space=pltpu.VMEM)
    f32 = jnp.float32
    return pl.pallas_call(
        factor_kernel,
        out_shape=(
            jax.ShapeDtypeStruct((128, 256), f32),
            jax.ShapeDtypeStruct((256, 256), f32),
        ),
        in_specs=[vmem, vmem],
        out_specs=(vmem, vmem),
        scratch_shapes=[pltpu.VMEM((256, 384), f32)],
        compiler_params=pltpu.CompilerParams(vmem_limit_bytes=40 << 20),
        name="factored",
    )(cross, sketch)


def on_device(precip, thresholds, bin_index, test_matrix):
    days = precip.shape[0] * lax.axis_size("tm")
    points_total = precip.shape[1] * lax.axis_size(PTS)
    rows = harmonic_basis(days)
    table = np.zeros((lax.axis_size("tm"), 32, precip.shape[0]), np.float32)
    table[:, : len(rows)] = rows.reshape(len(rows), -1, precip.shape[0]).swapaxes(0, 1)
    sketch_t, blocks = gathered(
        precip, table, test_matrix, bin_index.reshape(-1, 128), thresholds, points_total
    )
    return factored(blocks, sketch_t)


def solution(mesh):
    split = Mesh(mesh.devices.reshape(mesh.shape["tm"], 4, 8, 2), ("tm", *PTS))
    return jax.shard_map(
        on_device,
        mesh=split,
        in_specs=(P("tm", PTS), P(), P(PTS), P("tm", None)),
        out_specs=(P(PTS_TM, None), P()),
        check_vma=False,
    )
```

```python
import functools
import math

import jax
import jax.numpy as jnp
import numpy as np
from jax import lax
from jax.experimental import pallas as pl
from jax.experimental.pallas import tpu as pltpu
from jax.sharding import Mesh
from jax.sharding import PartitionSpec as P

HARM = 8
YEAR_DAYS = 365.25
ROWS = 2 * HARM + 1
PTS = ("pts_0", "pts_1", "pts_2")
PTS_TM = ("pts_0", "pts_1", "pts_2", "tm")
MESH = pl.DeviceIdType.MESH


def harmonic_basis(days):
    day = np.arange(days, dtype=np.float32)
    columns = [np.ones(days)]
    for order in range(1, HARM + 1):
        phase = (np.float32(2.0 * math.pi * order / YEAR_DAYS) * day).astype(np.float64)
        columns += [np.cos(phase), np.sin(phase)]
    table = np.stack(columns)
    return np.linalg.solve(np.linalg.cholesky(table @ table.T), table)


def terms(a):
    first = a.astype(jnp.bfloat16)
    rest = a - first.astype(jnp.float32)
    second = rest.astype(jnp.bfloat16)
    return first, second, (rest - second.astype(jnp.float32)).astype(jnp.bfloat16)


LEFT, RIGHT = (0, 0, 1, 1, 0, 2), (0, 1, 0, 1, 2, 0)


def left_of(parts, dim, count=6):
    return jnp.concatenate([parts[i] for i in LEFT[:count]], dim)


def right_of(parts, dim, count=6):
    return jnp.concatenate([parts[i] for i in RIGHT[:count]], dim)


def dot(a, b, dims=((1,), (0,))):
    return lax.dot_general(a, b, (dims, ((), ())), preferred_element_type=jnp.float32)


def gather_kernel(
    scale,
    precip_hbm,
    table_hbm,
    test_hbm,
    bins_hbm,
    thresholds_hbm,
    sketch_out,
    cross_out,
    *scratch,
):
    (
        precip,
        table,
        test,
        bins,
        thresholds,
        load_sem,
        test_t,
        table_t,
        proj_out,
        proj_in,
        coef,
        level,
        sketch,
        ring,
        cross,
        core_in,
        y_in,
        z_in,
        x_in,
        total,
        proj_sem,
        coef_sem,
        ring_sem,
        core_sem,
        y_sem,
        z_sem,
        x_sem,
        gather_sem,
        join_sem,
    ) = scratch
    y = lax.axis_index("tm")
    x = lax.axis_index("pts_0")
    z = lax.axis_index("pts_1")
    c = lax.axis_index("pts_2")
    n_y, n_x, n_z = (lax.axis_size(a) for a in ("tm", "pts_0", "pts_1"))
    sends = []


    def send(src, dst, sem, device):
        copy = pltpu.make_async_remote_copy(
            src_ref=src,
            dst_ref=dst,
            send_sem=sem.at[0],
            recv_sem=sem.at[1],
            device_id=device,
            device_id_type=MESH,
        )
        copy.start()
        sends.append(copy)
        return copy

    y_at = lambda o: lax.rem(y + o + n_y, n_y)
    x_at = lambda o: lax.rem(x + o + n_x, n_x)
    z_at = lambda o: lax.rem(z + o + n_z, n_z)

    coef[:, 16:] = jnp.zeros((n_y, 16, 128), jnp.float32)
    barrier = pltpu.get_barrier_semaphore()
    others = [{"tm": y_at(o)} for o in range(1, n_y)]
    others += [{"pts_0": x_at(o)} for o in range(1, n_x)]
    others += [{"pts_1": z_at(o)} for o in range(1, n_z)]
    others += [{"pts_2": 1 - c}]
    for other in others:
        pl.semaphore_signal(barrier, inc=1, device_id=other, device_id_type=MESH)

    loads = [
        pltpu.make_async_copy(src, dst, load_sem.at[i])
        for i, (src, dst) in enumerate(
            [
                (table_hbm.at[y], table),
                (precip_hbm, precip),
                (test_hbm, test),
                (bins_hbm, bins),
                (thresholds_hbm, thresholds),
            ]
        )
    ]
    for copy in loads:
        copy.start()

    loads[0].wait()
    loads[1].wait()
    one, two, three = terms(table[...])
    stack = jnp.concatenate([one, two, three], 0)
    for r in range(0, n_y, 2):
        data = terms(precip[:, 128 * r : 128 * (r + 2)])
        proj = dot(stack, data[0])
        more = dot(stack[:64], data[1])
        proj = proj[:32] + proj[32:64] + proj[64:] + more[:32] + more[32:] + dot(stack[:32], data[2])
        proj_out[r] = proj[:ROWS, :128]
        proj_out[r + 1] = proj[:ROWS, 128:]
    pl.semaphore_wait(barrier, len(others))
    arrivals = []
    for o in [4, 3, 5, 2, 6, 1, 7]:
        arrivals.append(send(proj_out.at[y_at(o)], proj_in.at[o], proj_sem.at[o], {"tm": y_at(o)}))
    for copy in loads[2:]:
        copy.wait()
    test_t[...] = left_of(terms(test[...].T), 1, TERMS)
    table_t[...] = left_of((one, two, three), 0).T
    found = bins[...]
    value = jnp.zeros(found.shape, jnp.float32)
    for k in range(thresholds.shape[0]):
        value = jnp.where(found == k, thresholds[k], value)
    level[...] = value
    for copy in arrivals:
        copy.wait_recv()
    own = proj_out[y]
    for o in range(1, n_y):
        own = own + proj_in[o]
    coef[y, :ROWS] = own
    mine = coef.at[y, pl.ds(0, ROWS)]
    arrivals = []
    for o in [4, 3, 5, 2, 6, 1, 7]:
        arrivals.append(send(mine, mine, coef_sem.at[o], {"tm": y_at(o)}))
    for copy in arrivals:
        copy.wait_recv()

    def partial(pair):
        join = lambda f: jnp.concatenate([f(y_at(o)) for o in pair], 1)
        found = join(lambda r: coef[r])
        fit = dot(table_t[...], right_of(terms(found), 0))
        data = join(lambda r: precip[:, pl.ds(pl.multiple_of(128 * r, 128), 128)])
        excess = jnp.maximum(data - fit - join(lambda r: level[pl.ds(r, 1), :]), 0.0)
        sums = dot(test_t[...], right_of(terms(excess), 0, TERMS))
        for i, o in enumerate(pair):
            sketch[o % n_y] = sums[:, 128 * i : 128 * i + 128]

    edges = [(h, s * a * t, s * b * t) for h, s in ((0, 1), (1, -1)) for side, t in ((LONG, -1), (SHORT, 1)) for a, b in side]
    level_of = lambda e: max((1 + level_of(f) for f in edges if f[0] == e[0] and f[2] == e[1]), default=0)
    edges.sort(key=lambda e: (level_of(e), -abs(e[1])))
    piece = 128 // PIECES
    moving = {}
    ready = set()

    def need(o):
        for pair in PAIRS:
            if o in [p % n_y for p in pair] and pair not in ready:
                partial(pair)
                ready.add(pair)

    def arrived(h, a, q):
        rows = pl.ds(128 * h + q * piece, piece)
        value = sketch[-a % n_y, rows]
        for i, e in enumerate(edges):
            if e[0] == h and e[2] == a:
                moving[i, q].wait_recv()
                value = value + ring[i, pl.ds(q * piece, piece)]
        return value

    for i, (h, a, b) in enumerate(edges):
        inner = [j for j, e in enumerate(edges) if e[0] == h and e[2] == a]
        need(-a % n_y)
        for q in range(PIECES):
            if inner:
                src = ring.at[inner[0], pl.ds(q * piece, piece)]
                src[...] = arrived(h, a, q)
            else:
                src = sketch.at[-a % n_y, pl.ds(128 * h + q * piece, piece)]
            moving[i, q] = send(
                src, ring.at[i, pl.ds(q * piece, piece)], ring_sem.at[i, q], {"tm": y_at(b - a)}
            )
        if i == EARLY:
            for o in range(n_y):
                need(o)
    for h in (0, 1):
        for q in range(PIECES):
            sketch_out[pl.ds(128 * h + q * piece, piece)] = arrived(h, 0, q)

    parts = terms(sketch_out[...])
    left = left_of(parts, 1)
    right = right_of(parts, 1)
    first = dot(left[:128], right[:128], ((1,), (1,))) * scale
    mixed = dot(left[:128], right[128:], ((1,), (1,))) * scale
    second = dot(left[128:], right[128:], ((1,), (1,))) * scale
    row = lax.broadcasted_iota(jnp.int32, (128, 128), 0)
    lane = lax.broadcasted_iota(jnp.int32, (128, 128), 1)
    cross[0, :, :16] = mixed.reshape(n_y, 16, 128)
    cross[1, :, :16] = jnp.where(row <= lane, first, second).reshape(n_y, 16, 128)
    cross[:, :, 16:] = jnp.zeros((2, n_y, 1, 128), jnp.float32)
    cross[1, 0, 16:] = jnp.sum(jnp.where(row == lane, second, 0.0), axis=0, keepdims=True)
    copy = send(cross.at[1 - c], core_in, core_sem, {"pts_2": 1 - c})
    copy.wait_recv()
    core_in[...] += cross[c]
    arrivals = []
    for o in [4, 3, 5, 2, 6, 1, 7]:
        arrivals.append(send(core_in.at[y_at(o)], y_in.at[o], y_sem.at[o], {"tm": y_at(o)}))
    for copy in arrivals:
        copy.wait_recv()
    own = core_in[y]
    for o in range(1, n_y):
        own = own + y_in[o]
    z_in[z] = own
    arrivals = []
    for o in [4, 3, 5, 2, 6, 1, 7]:
        arrivals.append(send(z_in.at[z], z_in.at[z], z_sem.at[o], {"pts_1": z_at(o)}))
    for copy in arrivals:
        copy.wait_recv()
    own = z_in[0]
    for o in range(1, n_z):
        own = own + z_in[o]
    x_in[x] = own
    arrivals = []
    for o in [2, 1, 3]:
        arrivals.append(send(x_in.at[x], x_in.at[x], x_sem.at[o], {"pts_0": x_at(o)}))
    for copy in arrivals:
        copy.wait_recv()
    own = x_in[0]
    for o in range(1, n_x):
        own = own + x_in[o]
    total[c, y] = own
    place = total.at[c, y]
    arrivals = []
    for o in [4, 3, 5, 2, 6, 1, 7]:
        arrivals.append(send(place, place, gather_sem.at[o], {"tm": y_at(o)}))
    for copy in arrivals:
        copy.wait_recv()
    place = total.at[c]
    send(place, place, join_sem, {"pts_2": 1 - c}).wait_recv()
    both = total[1, :, :16].reshape(128, 128)
    turned = both.T
    cross_out[:128] = jnp.where(row <= lane, both, turned)
    cross_out[128:256] = total[0, :, :16].reshape(128, 128)
    cross_out[256:] = jnp.where(row == lane, total[1, 0, 16:], jnp.where(row > lane, both, turned))
    for copy in sends:
        copy.wait_send()


PIECES = 2
TERMS = 3
PAIRS = ((4, 3), (-3, 2), (-2, 1), (-1, 0))
EARLY = 5
LONG = ((4, 2), (3, 2), (2, 1), (1, 0))
SHORT = ((3, 2), (2, 1), (1, 0))


def gathered(precip, table, test, bins, thresholds, points_total):
    vmem = pl.BlockSpec(memory_space=pltpu.VMEM)
    hbm = pl.BlockSpec(memory_space=pltpu.HBM)
    f32 = jnp.float32
    dma = pltpu.SemaphoreType.DMA
    operands = (precip, table, test, bins, thresholds)
    return pl.pallas_call(
        functools.partial(gather_kernel, 1.0 / points_total),
        out_shape=(
            jax.ShapeDtypeStruct((256, 128), f32),
            jax.ShapeDtypeStruct((384, 128), f32),
        ),
        in_specs=[hbm] * 5,
        out_specs=(vmem, vmem),
        scratch_shapes=[
            pltpu.VMEM(precip.shape, f32),
            pltpu.VMEM(table.shape[1:], f32),
            pltpu.VMEM(test.shape, f32),
            pltpu.VMEM(bins.shape, jnp.int32),
            pltpu.SMEM(thresholds.shape, f32),
            dma((5,)),
            pltpu.VMEM((256, 256 * TERMS), jnp.bfloat16),
            pltpu.VMEM((256, 192), jnp.bfloat16),
            pltpu.VMEM((8, ROWS, 128), f32),
            pltpu.VMEM((8, ROWS, 128), f32),
            pltpu.VMEM((8, 32, 128), f32),
            pltpu.VMEM((8, 128), f32),
            pltpu.VMEM((8, 256, 128), f32),
            pltpu.VMEM((14, 128, 128), f32),
            pltpu.VMEM((2, 8, 17, 128), f32),
            pltpu.VMEM((8, 17, 128), f32),
            pltpu.VMEM((8, 17, 128), f32),
            pltpu.VMEM((8, 17, 128), f32),
            pltpu.VMEM((4, 17, 128), f32),
            pltpu.VMEM((2, 8, 17, 128), f32),
            dma((8, 2)),
            dma((8, 2)),
            dma((14, PIECES, 2)),
            dma((2,)),
            dma((8, 2)),
            dma((8, 2)),
            dma((4, 2)),
            dma((8, 2)),
            dma((2,)),
        ],
        compiler_params=pltpu.CompilerParams(
            collective_id=0, has_side_effects=True, vmem_limit_bytes=40 << 20
        ),
        name="gathered",
    )(*(pltpu.with_memory_space_constraint(a, pltpu.HBM) for a in operands))


BLOCK = 32
STRIP = 16


def factor_kernel(cross, sketch, basis_out, factor_out, work):
    factor_out[128:, :128] = jnp.zeros((128, 128), jnp.float32)
    sub = lax.broadcasted_iota(jnp.int32, (8, 128), 0)
    lane = lax.broadcasted_iota(jnp.int32, (8, 128), 1)
    wide = lambda row: jnp.broadcast_to(row, (8, 128))
    groups = BLOCK // 8

    def source(low, high, u):
        if u == 2:
            return sketch[low:high]
        return cross[128 * u + low : 128 * u + high] if low < 128 else cross[128 + low : 128 + high]

    for first in range(0, 256, BLOCK):
        tile, start = first // 128, first % 128
        tiles = range(tile, 3)
        rows = {}
        for g in range(groups):
            low = first + 8 * g
            for u in tiles:
                rows[g, u] = (
                    work[low : low + 8, 128 * u : 128 * u + 128] if first else source(low, low + 8, u)
                )
        root = {g: jnp.zeros((8, 128), jnp.float32) for g in range(groups)}
        for open_at in range(0, BLOCK, STRIP):
            strip = range(open_at, open_at + STRIP)
            column = {
                (j, h): wide(rows[h, tile][:, start + j : start + j + 1])
                for j in strip
                for h in range(j // 8, groups)
            }
            for j in strip:
                g, i = divmod(j, 8)
                pivot = wide(column[j, g][i : i + 1])
                inverse = 1.0 / pivot
                root[g] = jnp.where(sub == i, lax.rsqrt(pivot), root[g])
                ratio = {h: column[j, h] * inverse for h in range(g, groups)}
                for k in range(j + 1, strip.stop):
                    value = wide(column[j, k // 8][k % 8 : k % 8 + 1])
                    for h in range(k // 8, groups):
                        column[k, h] = column[k, h] - ratio[h] * value
                ratio[g] = jnp.where(sub > i, ratio[g], 0.0)
                for u in tiles:
                    row = wide(rows[g, u][i : i + 1])
                    for h in range(g if i < 7 else g + 1, groups):
                        rows[h, u] = rows[h, u] - ratio[h] * row
        done = {}
        for g in range(groups):
            place = slice(first + 8 * g, first + 8 * g + 8)
            for u in tiles:
                value = rows[g, u] * root[g]
                if u == tile:
                    value = jnp.where(lane >= start + 8 * g + sub, value, 0.0)
                done[g, u] = value
                if u < 2:
                    factor_out[place, 128 * u : 128 * u + 128] = value
                else:
                    work[place, 256:] = value
        after = first + BLOCK
        if after >= 256:
            break
        base = 128 * tile
        panel = jnp.concatenate(
            [jnp.concatenate([done[g, u] for u in tiles], 1) for g in range(groups)], 0
        )
        parts = terms(panel)
        left = left_of(parts, 0)[:, : 256 - base].T
        right = right_of(parts, 0)
        ends = sorted({after, after + BLOCK, max(after, 128), 256})
        for low, high in zip(ends, ends[1:]):
            edge = 128 * (low // 128)
            change = dot(left[low - base : high - base], right[:, edge - base :])
            for u in range(edge // 128, 3):
                old = work[low:high, 128 * u : 128 * u + 128] if first else source(low, high, u)
                at = 128 * u - edge
                work[low:high, 128 * u : 128 * u + 128] = old - change[:, at : at + 128]
    basis_out[:, :128] = work[:128, 256:].T
    basis_out[:, 128:] = work[128:, 256:].T


def factored(cross, sketch):
    vmem = pl.BlockSpec(memory_space=pltpu.VMEM)
    f32 = jnp.float32
    return pl.pallas_call(
        factor_kernel,
        out_shape=(
            jax.ShapeDtypeStruct((128, 256), f32),
            jax.ShapeDtypeStruct((256, 256), f32),
        ),
        in_specs=[vmem, vmem],
        out_specs=(vmem, vmem),
        scratch_shapes=[pltpu.VMEM((256, 384), f32)],
        compiler_params=pltpu.CompilerParams(vmem_limit_bytes=40 << 20),
        name="factored",
    )(cross, sketch)


def on_device(precip, thresholds, bin_index, test_matrix):
    days = precip.shape[0] * lax.axis_size("tm")
    points_total = precip.shape[1] * lax.axis_size(PTS)
    rows = harmonic_basis(days)
    table = np.zeros((lax.axis_size("tm"), 32, precip.shape[0]), np.float32)
    table[:, : len(rows)] = rows.reshape(len(rows), -1, precip.shape[0]).swapaxes(0, 1)
    sketch_t, blocks = gathered(
        precip, table, test_matrix, bin_index.reshape(-1, 128), thresholds, points_total
    )
    return factored(blocks, sketch_t)


def solution(mesh):
    split = Mesh(mesh.devices.reshape(mesh.shape["tm"], 4, 8, 2), ("tm", *PTS))
    return jax.shard_map(
        on_device,
        mesh=split,
        in_specs=(P("tm", PTS), P(), P(PTS), P("tm", None)),
        out_specs=(P(PTS_TM, None), P()),
        check_vma=False,
    )
```

```python
import functools
import math

import jax
import jax.numpy as jnp
import numpy as np
from jax import lax
from jax.experimental import pallas as pl
from jax.experimental.pallas import tpu as pltpu
from jax.sharding import Mesh
from jax.sharding import PartitionSpec as P

HARM = 8
YEAR_DAYS = 365.25
ROWS = 2 * HARM + 1
PTS = ("pts_0", "pts_1", "pts_2")
PTS_TM = ("pts_0", "pts_1", "pts_2", "tm")
MESH = pl.DeviceIdType.MESH


def harmonic_basis(days):
    day = np.arange(days, dtype=np.float32)
    columns = [np.ones(days)]
    for order in range(1, HARM + 1):
        phase = (np.float32(2.0 * math.pi * order / YEAR_DAYS) * day).astype(np.float64)
        columns += [np.cos(phase), np.sin(phase)]
    table = np.stack(columns)
    return np.linalg.solve(np.linalg.cholesky(table @ table.T), table)


def terms(a):
    first = a.astype(jnp.bfloat16)
    rest = a - first.astype(jnp.float32)
    second = rest.astype(jnp.bfloat16)
    return first, second, (rest - second.astype(jnp.float32)).astype(jnp.bfloat16)


LEFT, RIGHT = (0, 0, 1, 1, 0, 2), (0, 1, 0, 1, 2, 0)


def left_of(parts, dim, count=6):
    return jnp.concatenate([parts[i] for i in LEFT[:count]], dim)


def right_of(parts, dim, count=6):
    return jnp.concatenate([parts[i] for i in RIGHT[:count]], dim)


def dot(a, b, dims=((1,), (0,))):
    return lax.dot_general(a, b, (dims, ((), ())), preferred_element_type=jnp.float32)


def gather_kernel(
    scale,
    precip_hbm,
    table_hbm,
    test_hbm,
    bins_hbm,
    thresholds_hbm,
    sketch_out,
    cross_out,
    *scratch,
):
    (
        precip,
        table,
        test,
        bins,
        thresholds,
        load_sem,
        test_t,
        table_t,
        proj_out,
        proj_in,
        coef,
        level,
        sketch,
        ring,
        cross,
        core_in,
        y_in,
        z_in,
        x_in,
        total,
        proj_sem,
        coef_sem,
        ring_sem,
        core_sem,
        y_sem,
        z_sem,
        x_sem,
        gather_sem,
        join_sem,
    ) = scratch
    y = lax.axis_index("tm")
    x = lax.axis_index("pts_0")
    z = lax.axis_index("pts_1")
    c = lax.axis_index("pts_2")
    n_y, n_x, n_z = (lax.axis_size(a) for a in ("tm", "pts_0", "pts_1"))
    sends = []

    def send(src, dst, sem, device):
        copy = pltpu.make_async_remote_copy(
            src_ref=src,
            dst_ref=dst,
            send_sem=sem.at[0],
            recv_sem=sem.at[1],
            device_id=device,
            device_id_type=MESH,
        )
        copy.start()
        sends.append(copy)
        return copy

    y_at = lambda o: lax.rem(y + o + n_y, n_y)
    x_at = lambda o: lax.rem(x + o + n_x, n_x)
    z_at = lambda o: lax.rem(z + o + n_z, n_z)

    coef[:, 16:] = jnp.zeros((n_y, 16, 128), jnp.float32)
    barrier = pltpu.get_barrier_semaphore()
    others = [{"tm": y_at(o)} for o in FAR]
    others += [{"pts_0": x_at(o)} for o in range(1, n_x)]
    others += [{"pts_1": z_at(o)} for o in FAR]
    others += [{"pts_2": 1 - c}]
    for other in others:
        pl.semaphore_signal(barrier, inc=1, device_id=other, device_id_type=MESH)

    loads = [
        pltpu.make_async_copy(src, dst, load_sem.at[i])
        for i, (src, dst) in enumerate(
            [
                (table_hbm.at[y], table),
                (precip_hbm, precip),
                (test_hbm, test),
                (bins_hbm, bins),
                (thresholds_hbm, thresholds),
            ]
        )
    ]
    for copy in loads:
        copy.start()

    loads[0].wait()
    loads[1].wait()
    one, two, three = terms(table[...])
    stack = jnp.concatenate([one, two, three], 0)
    for r in range(0, n_y, 2):
        data = terms(precip[:, 128 * r : 128 * (r + 2)])
        proj = dot(stack, data[0])
        more = dot(stack[:64], data[1])
        proj = proj[:32] + proj[32:64] + proj[64:] + more[:32] + more[32:] + dot(stack[:32], data[2])
        proj_out[r] = proj[:ROWS, :128]
        proj_out[r + 1] = proj[:ROWS, 128:]
    pl.semaphore_wait(barrier, len(others))
    arrivals = []
    for o in FAR:
        arrivals.append(send(proj_out.at[y_at(o)], proj_in.at[o], proj_sem.at[o], {"tm": y_at(o)}))
    for copy in loads[2:]:
        copy.wait()
    test_t[...] = left_of(terms(test[...].T), 1, TERMS)
    table_t[...] = left_of((one, two, three), 0).T
    found = bins[...]
    value = jnp.zeros(found.shape, jnp.float32)
    for k in range(thresholds.shape[0]):
        value = jnp.where(found == k, thresholds[k], value)
    level[...] = value
    for copy in arrivals:
        copy.wait_recv()
    own = proj_out[y]
    for o in range(1, n_y):
        own = own + proj_in[o]
    coef[y, :ROWS] = own
    mine = coef.at[y, pl.ds(0, ROWS)]
    arrivals = []
    for o in FAR:
        arrivals.append(send(mine, mine, coef_sem.at[o], {"tm": y_at(o)}))
    for copy in arrivals:
        copy.wait_recv()

    def partial(pair):
        join = lambda f: jnp.concatenate([f(y_at(o)) for o in pair], 1)
        found = join(lambda r: coef[r])
        fit = dot(table_t[...], right_of(terms(found), 0))
        data = join(lambda r: precip[:, pl.ds(pl.multiple_of(128 * r, 128), 128)])
        excess = jnp.maximum(data - fit - join(lambda r: level[pl.ds(r, 1), :]), 0.0)
        sums = dot(test_t[...], right_of(terms(excess), 0, TERMS))
        for i, o in enumerate(pair):
            sketch[o % n_y] = sums[:, 128 * i : 128 * i + 128]

    edges = [(h, s * a * t, s * b * t) for h, s in ((0, 1), (1, -1)) for side, t in ((LONG, -1), (SHORT, 1)) for a, b in side]
    level_of = lambda e: max((1 + level_of(f) for f in edges if f[0] == e[0] and f[2] == e[1]), default=0)
    edges.sort(key=lambda e: (level_of(e), -abs(e[1])))
    piece = 128 // PIECES
    moving = {}

    partial(FIRST)

    def arrived(h, a, q):
        rows = pl.ds(128 * h + q * piece, piece)
        value = sketch[-a % n_y, rows]
        for i, e in enumerate(edges):
            if e[0] == h and e[2] == a:
                moving[i, q].wait_recv()
                value = value + ring[i, pl.ds(q * piece, piece)]
        return value

    for i, (h, a, b) in enumerate(edges):
        inner = [j for j, e in enumerate(edges) if e[0] == h and e[2] == a]
        if i == sum(level_of(e) == 0 for e in edges):
            for chunks in LATER:
                partial(chunks)
        for q in range(PIECES):
            if inner:
                src = ring.at[inner[0], pl.ds(q * piece, piece)]
                src[...] = arrived(h, a, q)
            else:
                src = sketch.at[-a % n_y, pl.ds(128 * h + q * piece, piece)]
            moving[i, q] = send(
                src, ring.at[i, pl.ds(q * piece, piece)], ring_sem.at[i, q], {"tm": y_at(b - a)}
            )
    for h in (0, 1):
        for q in range(PIECES):
            sketch_out[pl.ds(128 * h + q * piece, piece)] = arrived(h, 0, q)

    parts = terms(sketch_out[...])
    left = left_of(parts, 1)
    right = right_of(parts, 1)
    first = dot(left[:128], right[:128], ((1,), (1,))) * scale
    mixed = dot(left[:128], right[128:], ((1,), (1,))) * scale
    second = dot(left[128:], right[128:], ((1,), (1,))) * scale
    row = lax.broadcasted_iota(jnp.int32, (128, 128), 0)
    lane = lax.broadcasted_iota(jnp.int32, (128, 128), 1)
    cross[0, :, :16] = mixed.reshape(n_y, 16, 128)
    cross[1, :, :16] = jnp.where(row <= lane, first, second).reshape(n_y, 16, 128)
    cross[:, :, 16:] = jnp.zeros((2, n_y, 1, 128), jnp.float32)
    cross[1, 0, 16:] = jnp.sum(jnp.where(row == lane, second, 0.0), axis=0, keepdims=True)
    copy = send(cross.at[1 - c], core_in, core_sem, {"pts_2": 1 - c})
    copy.wait_recv()
    core_in[...] += cross[c]
    arrivals = []
    for o in FAR:
        arrivals.append(send(core_in.at[y_at(o)], y_in.at[o], y_sem.at[o], {"tm": y_at(o)}))
    for copy in arrivals:
        copy.wait_recv()
    own = core_in[y]
    for o in range(1, n_y):
        own = own + y_in[o]
    z_in[z] = own
    arrivals = []
    for o in FAR:
        arrivals.append(send(z_in.at[z], z_in.at[z], z_sem.at[o], {"pts_1": z_at(o)}))
    for copy in arrivals:
        copy.wait_recv()
    own = z_in[0]
    for o in range(1, n_z):
        own = own + z_in[o]
    x_in[x] = own
    arrivals = []
    for o in [2, 1, 3]:
        arrivals.append(send(x_in.at[x], x_in.at[x], x_sem.at[o], {"pts_0": x_at(o)}))
    for copy in arrivals:
        copy.wait_recv()
    own = x_in[0]
    for o in range(1, n_x):
        own = own + x_in[o]
    total[c, y] = own
    place = total.at[c, y]
    arrivals = []
    for o in FAR:
        arrivals.append(send(place, place, gather_sem.at[o], {"tm": y_at(o)}))
    for copy in arrivals:
        copy.wait_recv()
    place = total.at[c]
    send(place, place, join_sem, {"pts_2": 1 - c}).wait_recv()
    both = total[1, :, :16].reshape(128, 128)
    turned = both.T
    cross_out[:128] = jnp.where(row <= lane, both, turned)
    cross_out[128:256] = total[0, :, :16].reshape(128, 128)
    cross_out[256:] = jnp.where(row == lane, total[1, 0, 16:], jnp.where(row > lane, both, turned))
    for copy in sends:
        copy.wait_send()


FAR = (4, 3, 5, 2, 6, 1, 7)
PIECES = 2
TERMS = 3
FIRST = (4, 3, -3)
LATER = ((2, -2), (1, -1), (0,))
LONG = ((4, 2), (3, 2), (2, 1), (1, 0))
SHORT = ((3, 2), (2, 1), (1, 0))


def gathered(precip, table, test, bins, thresholds, points_total):
    vmem = pl.BlockSpec(memory_space=pltpu.VMEM)
    hbm = pl.BlockSpec(memory_space=pltpu.HBM)
    f32 = jnp.float32
    dma = pltpu.SemaphoreType.DMA
    operands = (precip, table, test, bins, thresholds)
    return pl.pallas_call(
        functools.partial(gather_kernel, 1.0 / points_total),
        out_shape=(
            jax.ShapeDtypeStruct((256, 128), f32),
            jax.ShapeDtypeStruct((384, 128), f32),
        ),
        in_specs=[hbm] * 5,
        out_specs=(vmem, vmem),
        scratch_shapes=[
            pltpu.VMEM(precip.shape, f32),
            pltpu.VMEM(table.shape[1:], f32),
            pltpu.VMEM(test.shape, f32),
            pltpu.VMEM(bins.shape, jnp.int32),
            pltpu.SMEM(thresholds.shape, f32),
            dma((5,)),
            pltpu.VMEM((256, 256 * TERMS), jnp.bfloat16),
            pltpu.VMEM((256, 192), jnp.bfloat16),
            pltpu.VMEM((8, ROWS, 128), f32),
            pltpu.VMEM((8, ROWS, 128), f32),
            pltpu.VMEM((8, 32, 128), f32),
            pltpu.VMEM((8, 128), f32),
            pltpu.VMEM((8, 256, 128), f32),
            pltpu.VMEM((14, 128, 128), f32),
            pltpu.VMEM((2, 8, 17, 128), f32),
            pltpu.VMEM((8, 17, 128), f32),
            pltpu.VMEM((8, 17, 128), f32),
            pltpu.VMEM((8, 17, 128), f32),
            pltpu.VMEM((4, 17, 128), f32),
            pltpu.VMEM((2, 8, 17, 128), f32),
            dma((8, 2)),
            dma((8, 2)),
            dma((14, PIECES, 2)),
            dma((2,)),
            dma((8, 2)),
            dma((8, 2)),
            dma((4, 2)),
            dma((8, 2)),
            dma((2,)),
        ],
        compiler_params=pltpu.CompilerParams(
            collective_id=0, has_side_effects=True, vmem_limit_bytes=40 << 20
        ),
        name="gathered",
    )(*(pltpu.with_memory_space_constraint(a, pltpu.HBM) for a in operands))


BLOCK = 32
STRIP = 16


def factor_kernel(cross, sketch, basis_out, factor_out, work):
    factor_out[128:, :128] = jnp.zeros((128, 128), jnp.float32)
    sub = lax.broadcasted_iota(jnp.int32, (8, 128), 0)
    lane = lax.broadcasted_iota(jnp.int32, (8, 128), 1)
    wide = lambda row: jnp.broadcast_to(row, (8, 128))
    groups = BLOCK // 8

    def source(low, high, u):
        if u == 2:
            return sketch[low:high]
        return cross[128 * u + low : 128 * u + high] if low < 128 else cross[128 + low : 128 + high]

    for first in range(0, 256, BLOCK):
        tile, start = first // 128, first % 128
        tiles = range(tile, 3)
        rows = {}
        for g in range(groups):
            low = first + 8 * g
            for u in tiles:
                rows[g, u] = (
                    work[low : low + 8, 128 * u : 128 * u + 128] if first else source(low, low + 8, u)
                )
        root = {g: jnp.zeros((8, 128), jnp.float32) for g in range(groups)}
        for open_at in range(0, BLOCK, STRIP):
            strip = range(open_at, open_at + STRIP)
            column = {
                (j, h): wide(rows[h, tile][:, start + j : start + j + 1])
                for j in strip
                for h in range(j // 8, groups)
            }
            for j in strip:
                g, i = divmod(j, 8)
                pivot = wide(column[j, g][i : i + 1])
                inverse = 1.0 / pivot
                root[g] = jnp.where(sub == i, lax.rsqrt(pivot), root[g])
                ratio = {h: column[j, h] * inverse for h in range(g, groups)}
                for k in range(j + 1, strip.stop):
                    value = wide(column[j, k // 8][k % 8 : k % 8 + 1])
                    for h in range(k // 8, groups):
                        column[k, h] = column[k, h] - ratio[h] * value
                ratio[g] = jnp.where(sub > i, ratio[g], 0.0)
                for u in tiles:
                    row = wide(rows[g, u][i : i + 1])
                    for h in range(g if i < 7 else g + 1, groups):
                        rows[h, u] = rows[h, u] - ratio[h] * row
        done = {}
        for g in range(groups):
            place = slice(first + 8 * g, first + 8 * g + 8)
            for u in tiles:
                value = rows[g, u] * root[g]
                if u == tile:
                    value = jnp.where(lane >= start + 8 * g + sub, value, 0.0)
                done[g, u] = value
                if u < 2:
                    factor_out[place, 128 * u : 128 * u + 128] = value
                else:
                    work[place, 256:] = value
        after = first + BLOCK
        if after >= 256:
            break
        base = 128 * tile
        panel = jnp.concatenate(
            [jnp.concatenate([done[g, u] for u in tiles], 1) for g in range(groups)], 0
        )
        parts = terms(panel)
        left = left_of(parts, 0)[:, : 256 - base].T
        right = right_of(parts, 0)
        ends = sorted({after, after + BLOCK, max(after, 128), 256})
        for low, high in zip(ends, ends[1:]):
            edge = 128 * (low // 128)
            change = dot(left[low - base : high - base], right[:, edge - base :])
            for u in range(edge // 128, 3):
                old = work[low:high, 128 * u : 128 * u + 128] if first else source(low, high, u)
                at = 128 * u - edge
                work[low:high, 128 * u : 128 * u + 128] = old - change[:, at : at + 128]
    basis_out[:, :128] = work[:128, 256:].T
    basis_out[:, 128:] = work[128:, 256:].T


def factored(cross, sketch):
    vmem = pl.BlockSpec(memory_space=pltpu.VMEM)
    f32 = jnp.float32
    return pl.pallas_call(
        factor_kernel,
        out_shape=(
            jax.ShapeDtypeStruct((128, 256), f32),
            jax.ShapeDtypeStruct((256, 256), f32),
        ),
        in_specs=[vmem, vmem],
        out_specs=(vmem, vmem),
        scratch_shapes=[pltpu.VMEM((256, 384), f32)],
        compiler_params=pltpu.CompilerParams(vmem_limit_bytes=40 << 20),
        name="factored",
    )(cross, sketch)


def on_device(precip, thresholds, bin_index, test_matrix):
    days = precip.shape[0] * lax.axis_size("tm")
    points_total = precip.shape[1] * lax.axis_size(PTS)
    rows = harmonic_basis(days)
    table = np.zeros((lax.axis_size("tm"), 32, precip.shape[0]), np.float32)
    table[:, : len(rows)] = rows.reshape(len(rows), -1, precip.shape[0]).swapaxes(0, 1)
    sketch_t, blocks = gathered(
        precip, table, test_matrix, bin_index.reshape(-1, 128), thresholds, points_total
    )
    return factored(blocks, sketch_t)


def solution(mesh):
    split = Mesh(mesh.devices.reshape(mesh.shape["tm"], 4, 8, 2), ("tm", *PTS))
    return jax.shard_map(
        on_device,
        mesh=split,
        in_specs=(P("tm", PTS), P(), P(PTS), P("tm", None)),
        out_specs=(P(PTS_TM, None), P()),
        check_vma=False,
    )
```

```python
import functools
import math

import jax
import jax.numpy as jnp
import numpy as np
from jax import lax
from jax.experimental import pallas as pl
from jax.experimental.pallas import tpu as pltpu
from jax.sharding import Mesh
from jax.sharding import PartitionSpec as P

HARM = 8
YEAR_DAYS = 365.25
ROWS = 2 * HARM + 1
PTS = ("pts_0", "pts_1", "pts_2")
PTS_TM = ("pts_0", "pts_1", "pts_2", "tm")
MESH = pl.DeviceIdType.MESH


def harmonic_basis(days):
    day = np.arange(days, dtype=np.float32)
    columns = [np.ones(days)]
    for order in range(1, HARM + 1):
        phase = (np.float32(2.0 * math.pi * order / YEAR_DAYS) * day).astype(np.float64)
        columns += [np.cos(phase), np.sin(phase)]
    table = np.stack(columns)
    return np.linalg.solve(np.linalg.cholesky(table @ table.T), table)


def terms(a):
    first = a.astype(jnp.bfloat16)
    rest = a - first.astype(jnp.float32)
    second = rest.astype(jnp.bfloat16)
    return first, second, (rest - second.astype(jnp.float32)).astype(jnp.bfloat16)


LEFT, RIGHT = (0, 0, 1, 1, 0, 2), (0, 1, 0, 1, 2, 0)


def left_of(parts, dim, count=6):
    return jnp.concatenate([parts[i] for i in LEFT[:count]], dim)


def right_of(parts, dim, count=6):
    return jnp.concatenate([parts[i] for i in RIGHT[:count]], dim)


def dot(a, b, dims=((1,), (0,))):
    return lax.dot_general(a, b, (dims, ((), ())), preferred_element_type=jnp.float32)


def gather_kernel(
    scale,
    precip_hbm,
    table_hbm,
    test_hbm,
    bins_hbm,
    thresholds_hbm,
    sketch_out,
    cross_out,
    *scratch,
):
    (
        precip,
        table,
        test,
        bins,
        thresholds,
        load_sem,
        test_t,
        table_t,
        proj_out,
        proj_in,
        coef,
        level,
        sketch,
        ring,
        cross,
        core_in,
        y_in,
        z_in,
        x_in,
        total,
        proj_sem,
        coef_sem,
        ring_sem,
        core_sem,
        y_sem,
        z_sem,
        x_sem,
        gather_sem,
        join_sem,
    ) = scratch
    y = lax.axis_index("tm")
    x = lax.axis_index("pts_0")
    z = lax.axis_index("pts_1")
    c = lax.axis_index("pts_2")
    n_y, n_x, n_z = (lax.axis_size(a) for a in ("tm", "pts_0", "pts_1"))
    sends = []

    def send(src, dst, sem, device):
        copy = pltpu.make_async_remote_copy(
            src_ref=src,
            dst_ref=dst,
            send_sem=sem.at[0],
            recv_sem=sem.at[1],
            device_id=device,
            device_id_type=MESH,
        )
        copy.start()
        sends.append(copy)
        return copy

    y_at = lambda o: lax.rem(y + o + n_y, n_y)
    x_at = lambda o: lax.rem(x + o + n_x, n_x)
    z_at = lambda o: lax.rem(z + o + n_z, n_z)

    coef[:, 16:] = jnp.zeros((n_y, 16, 128), jnp.float32)
    barrier = pltpu.get_barrier_semaphore()
    others = [{"tm": y_at(o)} for o in FAR]
    others += [{"pts_0": x_at(o)} for o in range(1, n_x)]
    others += [{"pts_1": z_at(o)} for o in FAR]
    others += [{"pts_2": 1 - c}]
    for other in others:
        pl.semaphore_signal(barrier, inc=1, device_id=other, device_id_type=MESH)

    loads = [
        pltpu.make_async_copy(src, dst, load_sem.at[i])
        for i, (src, dst) in enumerate(
            [
                (table_hbm.at[y], table),
                (precip_hbm, precip),
                (test_hbm, test),
                (bins_hbm, bins),
                (thresholds_hbm, thresholds),
            ]
        )
    ]
    for copy in loads:
        copy.start()

    loads[0].wait()
    loads[1].wait()
    one, two, three = terms(table[...])
    stack = jnp.concatenate([one, two, three], 0)
    for r in range(0, n_y, 2):
        data = terms(precip[:, 128 * r : 128 * (r + 2)])
        proj = dot(stack, data[0])
        more = dot(stack[:64], data[1])
        proj = proj[:32] + proj[32:64] + proj[64:] + more[:32] + more[32:] + dot(stack[:32], data[2])
        proj_out[r] = proj[:ROWS, :128]
        proj_out[r + 1] = proj[:ROWS, 128:]
    pl.semaphore_wait(barrier, len(others))
    arrivals = []
    for o in FAR:
        arrivals.append(send(proj_out.at[y_at(o)], proj_in.at[o], proj_sem.at[o], {"tm": y_at(o)}))
    for copy in loads[2:]:
        copy.wait()
    test_t[...] = left_of(terms(test[...].T), 1, TERMS)
    table_t[...] = left_of((one, two, three), 0).T
    found = bins[...]
    value = jnp.zeros(found.shape, jnp.float32)
    for k in range(thresholds.shape[0]):
        value = jnp.where(found == k, thresholds[k], value)
    level[...] = value
    for copy in arrivals:
        copy.wait_recv()
    own = proj_out[y]
    for o in range(1, n_y):
        own = own + proj_in[o]
    coef[y, :ROWS] = own
    mine = coef.at[y, pl.ds(0, ROWS)]
    arrivals = []
    for o in FAR:
        arrivals.append(send(mine, mine, coef_sem.at[o], {"tm": y_at(o)}))
    for copy in arrivals:
        copy.wait_recv()

    def partial(pair):
        join = lambda f: jnp.concatenate([f(y_at(o)) for o in pair], 1)
        found = join(lambda r: coef[r])
        fit = dot(table_t[...], right_of(terms(found), 0))
        data = join(lambda r: precip[:, pl.ds(pl.multiple_of(128 * r, 128), 128)])
        excess = jnp.maximum(data - fit - join(lambda r: level[pl.ds(r, 1), :]), 0.0)
        sums = dot(test_t[...], right_of(terms(excess), 0, TERMS))
        for i, o in enumerate(pair):
            sketch[o % n_y] = sums[:, 128 * i : 128 * i + 128]

    edges = [(h, s * a * t, s * b * t) for h, s in ((0, 1), (1, -1)) for side, t in ((LONG, -1), (SHORT, 1)) for a, b in side]
    level_of = lambda e: max((1 + level_of(f) for f in edges if f[0] == e[0] and f[2] == e[1]), default=0)
    edges.sort(key=lambda e: (level_of(e), -abs(e[1])))
    piece = 128 // PIECES
    moving = {}

    partial(FIRST)

    def arrived(h, a, q):
        rows = pl.ds(128 * h + q * piece, piece)
        value = sketch[-a % n_y, rows]
        for i, e in enumerate(edges):
            if e[0] == h and e[2] == a:
                moving[i, q].wait_recv()
                value = value + ring[i, pl.ds(q * piece, piece)]
        return value

    for i, (h, a, b) in enumerate(edges):
        inner = [j for j, e in enumerate(edges) if e[0] == h and e[2] == a]
        if i == sum(level_of(e) == 0 for e in edges):
            for chunks in LATER:
                partial(chunks)
        for q in range(PIECES):
            if inner:
                src = ring.at[inner[0], pl.ds(q * piece, piece)]
                src[...] = arrived(h, a, q)
            else:
                src = sketch.at[-a % n_y, pl.ds(128 * h + q * piece, piece)]
            moving[i, q] = send(
                src, ring.at[i, pl.ds(q * piece, piece)], ring_sem.at[i, q], {"tm": y_at(b - a)}
            )
    for h in (0, 1):
        for q in range(PIECES):
            sketch_out[pl.ds(128 * h + q * piece, piece)] = arrived(h, 0, q)

    parts = terms(sketch_out[...])
    left = left_of(parts, 1)
    right = right_of(parts, 1)
    first = dot(left[:128], right[:128], ((1,), (1,))) * scale
    mixed = dot(left[:128], right[128:], ((1,), (1,))) * scale
    second = dot(left[128:], right[128:], ((1,), (1,))) * scale
    row = lax.broadcasted_iota(jnp.int32, (128, 128), 0)
    lane = lax.broadcasted_iota(jnp.int32, (128, 128), 1)
    cross[0, :, :16] = mixed.reshape(n_y, 16, 128)
    cross[1, :, :16] = jnp.where(row <= lane, first, second).reshape(n_y, 16, 128)
    cross[:, :, 16:] = jnp.zeros((2, n_y, 1, 128), jnp.float32)
    cross[1, 0, 16:] = jnp.sum(jnp.where(row == lane, second, 0.0), axis=0, keepdims=True)
    halves = {}
    for o in (*FAR, 0):
        r = y_at(o)
        halves[o] = send(cross.at[1 - c, r], core_in.at[r], core_sem.at[o], {"pts_2": 1 - c})
    arrivals = []
    for o in (*FAR, 0):
        halves[o].wait_recv()
        core_in[y_at(o)] += cross[c, y_at(o)]
        if o == 0:
            continue
        arrivals.append(send(core_in.at[y_at(o)], y_in.at[o], y_sem.at[o], {"tm": y_at(o)}))
    for copy in arrivals:
        copy.wait_recv()
    own = core_in[y]
    for o in range(1, n_y):
        own = own + y_in[o]
    z_in[z] = own
    arrivals = []
    for o in FAR:
        arrivals.append(send(z_in.at[z], z_in.at[z], z_sem.at[o], {"pts_1": z_at(o)}))
    for copy in arrivals:
        copy.wait_recv()
    own = z_in[0]
    for o in range(1, n_z):
        own = own + z_in[o]
    x_in[x] = own
    arrivals = []
    for o in [2, 1, 3]:
        arrivals.append(send(x_in.at[x], x_in.at[x], x_sem.at[o], {"pts_0": x_at(o)}))
    for copy in arrivals:
        copy.wait_recv()
    own = x_in[0]
    for o in range(1, n_x):
        own = own + x_in[o]
    total[c, y] = own
    place = total.at[c, y]
    arrivals = {}
    for o in FAR:
        arrivals[o] = send(place, place, gather_sem.at[o], {"tm": y_at(o)})
    joins = [send(place, place, join_sem.at[0], {"pts_2": 1 - c})]
    for o in (1, 7, 2, 6, 3, 5, 4):
        arrivals[o].wait_recv()
        place = total.at[c, y_at(-o)]
        joins.append(send(place, place, join_sem.at[o], {"pts_2": 1 - c}))
    for copy in joins:
        copy.wait_recv()
    both = total[1, :, :16].reshape(128, 128)
    turned = both.T
    cross_out[:128] = jnp.where(row <= lane, both, turned)
    cross_out[128:256] = total[0, :, :16].reshape(128, 128)
    cross_out[256:] = jnp.where(row == lane, total[1, 0, 16:], jnp.where(row > lane, both, turned))
    for copy in sends:
        copy.wait_send()


FAR = (4, 3, 5, 2, 6, 1, 7)
PIECES = 2
TERMS = 3
FIRST = (4, 3, -3)
LATER = ((2, -2), (1, -1), (0,))
LONG = ((4, 2), (3, 2), (2, 1), (1, 0))
SHORT = ((3, 2), (2, 1), (1, 0))


def gathered(precip, table, test, bins, thresholds, points_total):
    vmem = pl.BlockSpec(memory_space=pltpu.VMEM)
    hbm = pl.BlockSpec(memory_space=pltpu.HBM)
    f32 = jnp.float32
    dma = pltpu.SemaphoreType.DMA
    operands = (precip, table, test, bins, thresholds)
    return pl.pallas_call(
        functools.partial(gather_kernel, 1.0 / points_total),
        out_shape=(
            jax.ShapeDtypeStruct((256, 128), f32),
            jax.ShapeDtypeStruct((384, 128), f32),
        ),
        in_specs=[hbm] * 5,
        out_specs=(vmem, vmem),
        scratch_shapes=[
            pltpu.VMEM(precip.shape, f32),
            pltpu.VMEM(table.shape[1:], f32),
            pltpu.VMEM(test.shape, f32),
            pltpu.VMEM(bins.shape, jnp.int32),
            pltpu.SMEM(thresholds.shape, f32),
            dma((5,)),
            pltpu.VMEM((256, 256 * TERMS), jnp.bfloat16),
            pltpu.VMEM((256, 192), jnp.bfloat16),
            pltpu.VMEM((8, ROWS, 128), f32),
            pltpu.VMEM((8, ROWS, 128), f32),
            pltpu.VMEM((8, 32, 128), f32),
            pltpu.VMEM((8, 128), f32),
            pltpu.VMEM((8, 256, 128), f32),
            pltpu.VMEM((14, 128, 128), f32),
            pltpu.VMEM((2, 8, 17, 128), f32),
            pltpu.VMEM((8, 17, 128), f32),
            pltpu.VMEM((8, 17, 128), f32),
            pltpu.VMEM((8, 17, 128), f32),
            pltpu.VMEM((4, 17, 128), f32),
            pltpu.VMEM((2, 8, 17, 128), f32),
            dma((8, 2)),
            dma((8, 2)),
            dma((14, PIECES, 2)),
            dma((8, 2)),
            dma((8, 2)),
            dma((8, 2)),
            dma((4, 2)),
            dma((8, 2)),
            dma((8, 2)),
        ],
        compiler_params=pltpu.CompilerParams(
            collective_id=0, has_side_effects=True, vmem_limit_bytes=40 << 20
        ),
        name="gathered",
    )(*(pltpu.with_memory_space_constraint(a, pltpu.HBM) for a in operands))


BLOCK = 32
STRIP = 16


def factor_kernel(cross, sketch, basis_out, factor_out, work):
    factor_out[128:, :128] = jnp.zeros((128, 128), jnp.float32)
    sub = lax.broadcasted_iota(jnp.int32, (8, 128), 0)
    lane = lax.broadcasted_iota(jnp.int32, (8, 128), 1)
    wide = lambda row: jnp.broadcast_to(row, (8, 128))
    groups = BLOCK // 8

    def source(low, high, u):
        if u == 2:
            return sketch[low:high]
        return cross[128 * u + low : 128 * u + high] if low < 128 else cross[128 + low : 128 + high]

    for first in range(0, 256, BLOCK):
        tile, start = first // 128, first % 128
        tiles = range(tile, 3)
        rows = {}
        for g in range(groups):
            low = first + 8 * g
            for u in tiles:
                rows[g, u] = (
                    work[low : low + 8, 128 * u : 128 * u + 128] if first else source(low, low + 8, u)
                )
        root = {g: jnp.zeros((8, 128), jnp.float32) for g in range(groups)}
        for open_at in range(0, BLOCK, STRIP):
            strip = range(open_at, open_at + STRIP)
            column = {
                (j, h): wide(rows[h, tile][:, start + j : start + j + 1])
                for j in strip
                for h in range(j // 8, groups)
            }
            for j in strip:
                g, i = divmod(j, 8)
                pivot = wide(column[j, g][i : i + 1])
                inverse = 1.0 / pivot
                root[g] = jnp.where(sub == i, lax.rsqrt(pivot), root[g])
                ratio = {h: column[j, h] * inverse for h in range(g, groups)}
                for k in range(j + 1, strip.stop):
                    value = wide(column[j, k // 8][k % 8 : k % 8 + 1])
                    for h in range(k // 8, groups):
                        column[k, h] = column[k, h] - ratio[h] * value
                ratio[g] = jnp.where(sub > i, ratio[g], 0.0)
                for u in tiles:
                    row = wide(rows[g, u][i : i + 1])
                    for h in range(g if i < 7 else g + 1, groups):
                        rows[h, u] = rows[h, u] - ratio[h] * row
        done = {}
        for g in range(groups):
            place = slice(first + 8 * g, first + 8 * g + 8)
            for u in tiles:
                value = rows[g, u] * root[g]
                if u == tile:
                    value = jnp.where(lane >= start + 8 * g + sub, value, 0.0)
                done[g, u] = value
                if u < 2:
                    factor_out[place, 128 * u : 128 * u + 128] = value
                else:
                    work[place, 256:] = value
        after = first + BLOCK
        if after >= 256:
            break
        base = 128 * tile
        panel = jnp.concatenate(
            [jnp.concatenate([done[g, u] for u in tiles], 1) for g in range(groups)], 0
        )
        parts = terms(panel)
        left = left_of(parts, 0)[:, : 256 - base].T
        right = right_of(parts, 0)
        ends = sorted({after, after + BLOCK, max(after, 128), 256})
        for low, high in zip(ends, ends[1:]):
            edge = 128 * (low // 128)
            change = dot(left[low - base : high - base], right[:, edge - base :])
            for u in range(edge // 128, 3):
                old = work[low:high, 128 * u : 128 * u + 128] if first else source(low, high, u)
                at = 128 * u - edge
                work[low:high, 128 * u : 128 * u + 128] = old - change[:, at : at + 128]
    basis_out[:, :128] = work[:128, 256:].T
    basis_out[:, 128:] = work[128:, 256:].T


def factored(cross, sketch):
    vmem = pl.BlockSpec(memory_space=pltpu.VMEM)
    f32 = jnp.float32
    return pl.pallas_call(
        factor_kernel,
        out_shape=(
            jax.ShapeDtypeStruct((128, 256), f32),
            jax.ShapeDtypeStruct((256, 256), f32),
        ),
        in_specs=[vmem, vmem],
        out_specs=(vmem, vmem),
        scratch_shapes=[pltpu.VMEM((256, 384), f32)],
        compiler_params=pltpu.CompilerParams(vmem_limit_bytes=40 << 20),
        name="factored",
    )(cross, sketch)


def on_device(precip, thresholds, bin_index, test_matrix):
    days = precip.shape[0] * lax.axis_size("tm")
    points_total = precip.shape[1] * lax.axis_size(PTS)
    rows = harmonic_basis(days)
    table = np.zeros((lax.axis_size("tm"), 32, precip.shape[0]), np.float32)
    table[:, : len(rows)] = rows.reshape(len(rows), -1, precip.shape[0]).swapaxes(0, 1)
    sketch_t, blocks = gathered(
        precip, table, test_matrix, bin_index.reshape(-1, 128), thresholds, points_total
    )
    return factored(blocks, sketch_t)


def solution(mesh):
    split = Mesh(mesh.devices.reshape(mesh.shape["tm"], 4, 8, 2), ("tm", *PTS))
    return jax.shard_map(
        on_device,
        mesh=split,
        in_specs=(P("tm", PTS), P(), P(PTS), P("tm", None)),
        out_specs=(P(PTS_TM, None), P()),
        check_vma=False,
    )
```

```python
import functools
import math

import jax
import jax.numpy as jnp
import numpy as np
from jax import lax
from jax.experimental import pallas as pl
from jax.experimental.pallas import tpu as pltpu
from jax.sharding import Mesh
from jax.sharding import PartitionSpec as P

HARM = 8
YEAR_DAYS = 365.25
ROWS = 2 * HARM + 1
PTS = ("pts_0", "pts_1", "pts_2")
PTS_TM = ("pts_0", "pts_1", "pts_2", "tm")
MESH = pl.DeviceIdType.MESH


def harmonic_basis(days):
    day = np.arange(days, dtype=np.float32)
    columns = [np.ones(days)]
    for order in range(1, HARM + 1):
        phase = (np.float32(2.0 * math.pi * order / YEAR_DAYS) * day).astype(np.float64)
        columns += [np.cos(phase), np.sin(phase)]
    table = np.stack(columns)
    return np.linalg.solve(np.linalg.cholesky(table @ table.T), table)


def terms(a):
    first = a.astype(jnp.bfloat16)
    rest = a - first.astype(jnp.float32)
    second = rest.astype(jnp.bfloat16)
    return first, second, (rest - second.astype(jnp.float32)).astype(jnp.bfloat16)


LEFT, RIGHT = (0, 0, 1, 1, 0, 2), (0, 1, 0, 1, 2, 0)


def left_of(parts, dim, count=6):
    return jnp.concatenate([parts[i] for i in LEFT[:count]], dim)


def right_of(parts, dim, count=6):
    return jnp.concatenate([parts[i] for i in RIGHT[:count]], dim)


def dot(a, b, dims=((1,), (0,))):
    return lax.dot_general(a, b, (dims, ((), ())), preferred_element_type=jnp.float32)


def gather_kernel(
    scale,
    precip_hbm,
    table_hbm,
    test_hbm,
    bins_hbm,
    thresholds_hbm,
    sketch_out,
    cross_out,
    *scratch,
):
    (
        precip,
        table,
        test,
        bins,
        thresholds,
        load_sem,
        test_t,
        table_t,
        proj_out,
        proj_in,
        coef,
        level,
        sketch,
        ring,
        cross,
        core_in,
        y_in,
        z_in,
        x_in,
        total,
        proj_sem,
        coef_sem,
        ring_sem,
        core_sem,
        y_sem,
        z_sem,
        x_sem,
        gather_sem,
        join_sem,
    ) = scratch
    y = lax.axis_index("tm")
    x = lax.axis_index("pts_0")
    z = lax.axis_index("pts_1")
    c = lax.axis_index("pts_2")
    n_y, n_x, n_z = (lax.axis_size(a) for a in ("tm", "pts_0", "pts_1"))
    sends = []

    def send(src, dst, sem, device):
        copy = pltpu.make_async_remote_copy(
            src_ref=src,
            dst_ref=dst,
            send_sem=sem.at[0],
            recv_sem=sem.at[1],
            device_id=device,
            device_id_type=MESH,
        )
        copy.start()
        sends.append(copy)
        return copy

    y_at = lambda o: lax.rem(y + o + n_y, n_y)
    x_at = lambda o: lax.rem(x + o + n_x, n_x)
    z_at = lambda o: lax.rem(z + o + n_z, n_z)

    coef[:, 16:] = jnp.zeros((n_y, 16, 128), jnp.float32)
    barrier = pltpu.get_barrier_semaphore()
    others = [{"tm": y_at(o)} for o in FAR]
    others += [{"pts_0": x_at(o)} for o in range(1, n_x)]
    others += [{"pts_1": z_at(o)} for o in FAR]
    others += [{"pts_2": 1 - c}]
    for other in others:
        pl.semaphore_signal(barrier, inc=1, device_id=other, device_id_type=MESH)

    loads = [
        pltpu.make_async_copy(src, dst, load_sem.at[i])
        for i, (src, dst) in enumerate(
            [
                (table_hbm.at[y], table),
                (precip_hbm, precip),
                (test_hbm, test),
                (bins_hbm, bins),
                (thresholds_hbm, thresholds),
            ]
        )
    ]
    for copy in loads:
        copy.start()

    loads[0].wait()
    loads[1].wait()
    one, two, three = terms(table[...])
    stack = jnp.concatenate([one, two, three], 0)
    for r in range(0, n_y, 2):
        data = terms(precip[:, 128 * r : 128 * (r + 2)])
        proj = dot(stack, data[0])
        more = dot(stack[:64], data[1])
        proj = proj[:32] + proj[32:64] + proj[64:] + more[:32] + more[32:] + dot(stack[:32], data[2])
        proj_out[r] = proj[:ROWS, :128]
        proj_out[r + 1] = proj[:ROWS, 128:]
    pl.semaphore_wait(barrier, len(others))
    arrivals = []
    due = sends[:]
    sends.clear()
    for o in FAR:
        arrivals.append(send(proj_out.at[y_at(o)], proj_in.at[o], proj_sem.at[o], {"tm": y_at(o)}))
    for copy in loads[2:]:
        copy.wait()
    test_t[...] = left_of(terms(test[...].T), 1, TERMS)
    table_t[...] = left_of((one, two, three), 0).T
    found = bins[...]
    value = jnp.zeros(found.shape, jnp.float32)
    for k in range(thresholds.shape[0]):
        value = jnp.where(found == k, thresholds[k], value)
    level[...] = value
    for copy in due:
        copy.wait_send()
    for copy in arrivals:
        copy.wait_recv()
    own = proj_out[y]
    for o in range(1, n_y):
        own = own + proj_in[o]
    coef[y, :ROWS] = own
    mine = coef.at[y, pl.ds(0, ROWS)]
    arrivals = []
    due = sends[:]
    sends.clear()
    for o in FAR:
        arrivals.append(send(mine, mine, coef_sem.at[o], {"tm": y_at(o)}))
    for copy in due:
        copy.wait_send()
    for copy in arrivals:
        copy.wait_recv()

    def partial(pair):
        join = lambda f: jnp.concatenate([f(y_at(o)) for o in pair], 1)
        found = join(lambda r: coef[r])
        fit = dot(table_t[...], right_of(terms(found), 0))
        data = join(lambda r: precip[:, pl.ds(pl.multiple_of(128 * r, 128), 128)])
        excess = jnp.maximum(data - fit - join(lambda r: level[pl.ds(r, 1), :]), 0.0)
        sums = dot(test_t[...], right_of(terms(excess), 0, TERMS))
        for i, o in enumerate(pair):
            sketch[o % n_y] = sums[:, 128 * i : 128 * i + 128]

    edges = [(h, s * a * t, s * b * t) for h, s in ((0, 1), (1, -1)) for side, t in ((LONG, -1), (SHORT, 1)) for a, b in side]
    level_of = lambda e: max((1 + level_of(f) for f in edges if f[0] == e[0] and f[2] == e[1]), default=0)
    edges.sort(key=lambda e: (level_of(e), -abs(e[1])))
    piece = 128 // PIECES
    moving = {}

    partial(FIRST)

    def arrived(h, a, q):
        rows = pl.ds(128 * h + q * piece, piece)
        value = sketch[-a % n_y, rows]
        for i, e in enumerate(edges):
            if e[0] == h and e[2] == a:
                moving[i, q].wait_recv()
                value = value + ring[i, pl.ds(q * piece, piece)]
        return value

    for i, (h, a, b) in enumerate(edges):
        inner = [j for j, e in enumerate(edges) if e[0] == h and e[2] == a]
        if i == sum(level_of(e) == 0 for e in edges):
            for chunks in LATER:
                partial(chunks)
        for q in range(PIECES):
            if inner:
                src = ring.at[inner[0], pl.ds(q * piece, piece)]
                src[...] = arrived(h, a, q)
            else:
                src = sketch.at[-a % n_y, pl.ds(128 * h + q * piece, piece)]
            moving[i, q] = send(
                src, ring.at[i, pl.ds(q * piece, piece)], ring_sem.at[i, q], {"tm": y_at(b - a)}
            )
    for h in (0, 1):
        for q in range(PIECES):
            sketch_out[pl.ds(128 * h + q * piece, piece)] = arrived(h, 0, q)

    parts = terms(sketch_out[...])
    left = left_of(parts, 1)
    right = right_of(parts, 1)
    first = dot(left[:128], right[:128], ((1,), (1,))) * scale
    mixed = dot(left[:128], right[128:], ((1,), (1,))) * scale
    second = dot(left[128:], right[128:], ((1,), (1,))) * scale
    row = lax.broadcasted_iota(jnp.int32, (128, 128), 0)
    lane = lax.broadcasted_iota(jnp.int32, (128, 128), 1)
    cross[0, :, :16] = mixed.reshape(n_y, 16, 128)
    cross[1, :, :16] = jnp.where(row <= lane, first, second).reshape(n_y, 16, 128)
    cross[:, :, 16:] = jnp.zeros((2, n_y, 1, 128), jnp.float32)
    cross[1, 0, 16:] = jnp.sum(jnp.where(row == lane, second, 0.0), axis=0, keepdims=True)
    copy = send(cross.at[1 - c], core_in, core_sem, {"pts_2": 1 - c})
    copy.wait_recv()
    core_in[...] += cross[c]
    arrivals = []
    due = sends[:]
    sends.clear()
    for o in FAR:
        arrivals.append(send(core_in.at[y_at(o)], y_in.at[o], y_sem.at[o], {"tm": y_at(o)}))
    for copy in due:
        copy.wait_send()
    for copy in arrivals:
        copy.wait_recv()
    own = core_in[y]
    for o in range(1, n_y):
        own = own + y_in[o]
    z_in[z] = own
    arrivals = []
    due = sends[:]
    sends.clear()
    for o in FAR:
        arrivals.append(send(z_in.at[z], z_in.at[z], z_sem.at[o], {"pts_1": z_at(o)}))
    for copy in due:
        copy.wait_send()
    for copy in arrivals:
        copy.wait_recv()
    own = z_in[0]
    for o in range(1, n_z):
        own = own + z_in[o]
    x_in[x] = own
    arrivals = []
    due = sends[:]
    sends.clear()
    for o in [2, 1, 3]:
        arrivals.append(send(x_in.at[x], x_in.at[x], x_sem.at[o], {"pts_0": x_at(o)}))
    for copy in due:
        copy.wait_send()
    for copy in arrivals:
        copy.wait_recv()
    own = x_in[0]
    for o in range(1, n_x):
        own = own + x_in[o]
    total[c, y] = own
    place = total.at[c, y]
    arrivals = []
    due = sends[:]
    sends.clear()
    for o in FAR:
        arrivals.append(send(place, place, gather_sem.at[o], {"tm": y_at(o)}))
    for copy in due:
        copy.wait_send()
    for copy in arrivals:
        copy.wait_recv()
    place = total.at[c]
    send(place, place, join_sem, {"pts_2": 1 - c}).wait_recv()
    both = total[1, :, :16].reshape(128, 128)
    turned = both.T
    cross_out[:128] = jnp.where(row <= lane, both, turned)
    cross_out[128:256] = total[0, :, :16].reshape(128, 128)
    cross_out[256:] = jnp.where(row == lane, total[1, 0, 16:], jnp.where(row > lane, both, turned))
    for copy in sends:
        copy.wait_send()


FAR = (4, 3, 5, 2, 6, 1, 7)
PIECES = 2
TERMS = 3
FIRST = (4, 3, -3)
LATER = ((2, -2), (1, -1), (0,))
LONG = ((4, 2), (3, 2), (2, 1), (1, 0))
SHORT = ((3, 2), (2, 1), (1, 0))


def gathered(precip, table, test, bins, thresholds, points_total):
    vmem = pl.BlockSpec(memory_space=pltpu.VMEM)
    hbm = pl.BlockSpec(memory_space=pltpu.HBM)
    f32 = jnp.float32
    dma = pltpu.SemaphoreType.DMA
    operands = (precip, table, test, bins, thresholds)
    return pl.pallas_call(
        functools.partial(gather_kernel, 1.0 / points_total),
        out_shape=(
            jax.ShapeDtypeStruct((256, 128), f32),
            jax.ShapeDtypeStruct((384, 128), f32),
        ),
        in_specs=[hbm] * 5,
        out_specs=(vmem, vmem),
        scratch_shapes=[
            pltpu.VMEM(precip.shape, f32),
            pltpu.VMEM(table.shape[1:], f32),
            pltpu.VMEM(test.shape, f32),
            pltpu.VMEM(bins.shape, jnp.int32),
            pltpu.SMEM(thresholds.shape, f32),
            dma((5,)),
            pltpu.VMEM((256, 256 * TERMS), jnp.bfloat16),
            pltpu.VMEM((256, 192), jnp.bfloat16),
            pltpu.VMEM((8, ROWS, 128), f32),
            pltpu.VMEM((8, ROWS, 128), f32),
            pltpu.VMEM((8, 32, 128), f32),
            pltpu.VMEM((8, 128), f32),
            pltpu.VMEM((8, 256, 128), f32),
            pltpu.VMEM((14, 128, 128), f32),
            pltpu.VMEM((2, 8, 17, 128), f32),
            pltpu.VMEM((8, 17, 128), f32),
            pltpu.VMEM((8, 17, 128), f32),
            pltpu.VMEM((8, 17, 128), f32),
            pltpu.VMEM((4, 17, 128), f32),
            pltpu.VMEM((2, 8, 17, 128), f32),
            dma((8, 2)),
            dma((8, 2)),
            dma((14, PIECES, 2)),
            dma((2,)),
            dma((8, 2)),
            dma((8, 2)),
            dma((4, 2)),
            dma((8, 2)),
            dma((2,)),
        ],
        compiler_params=pltpu.CompilerParams(
            collective_id=0, has_side_effects=True, vmem_limit_bytes=40 << 20
        ),
        name="gathered",
    )(*(pltpu.with_memory_space_constraint(a, pltpu.HBM) for a in operands))


BLOCK = 32
STRIP = 16


def factor_kernel(cross, sketch, basis_out, factor_out, work):
    factor_out[128:, :128] = jnp.zeros((128, 128), jnp.float32)
    sub = lax.broadcasted_iota(jnp.int32, (8, 128), 0)
    lane = lax.broadcasted_iota(jnp.int32, (8, 128), 1)
    wide = lambda row: jnp.broadcast_to(row, (8, 128))
    groups = BLOCK // 8

    def source(low, high, u):
        if u == 2:
            return sketch[low:high]
        return cross[128 * u + low : 128 * u + high] if low < 128 else cross[128 + low : 128 + high]

    for first in range(0, 256, BLOCK):
        tile, start = first // 128, first % 128
        tiles = range(tile, 3)
        rows = {}
        for g in range(groups):
            low = first + 8 * g
            for u in tiles:
                rows[g, u] = (
                    work[low : low + 8, 128 * u : 128 * u + 128] if first else source(low, low + 8, u)
                )
        root = {g: jnp.zeros((8, 128), jnp.float32) for g in range(groups)}
        for open_at in range(0, BLOCK, STRIP):
            strip = range(open_at, open_at + STRIP)
            column = {
                (j, h): wide(rows[h, tile][:, start + j : start + j + 1])
                for j in strip
                for h in range(j // 8, groups)
            }
            for j in strip:
                g, i = divmod(j, 8)
                pivot = wide(column[j, g][i : i + 1])
                inverse = 1.0 / pivot
                root[g] = jnp.where(sub == i, lax.rsqrt(pivot), root[g])
                ratio = {h: column[j, h] * inverse for h in range(g, groups)}
                for k in range(j + 1, strip.stop):
                    value = wide(column[j, k // 8][k % 8 : k % 8 + 1])
                    for h in range(k // 8, groups):
                        column[k, h] = column[k, h] - ratio[h] * value
                ratio[g] = jnp.where(sub > i, ratio[g], 0.0)
                for u in tiles:
                    row = wide(rows[g, u][i : i + 1])
                    for h in range(g if i < 7 else g + 1, groups):
                        rows[h, u] = rows[h, u] - ratio[h] * row
        done = {}
        for g in range(groups):
            place = slice(first + 8 * g, first + 8 * g + 8)
            for u in tiles:
                value = rows[g, u] * root[g]
                if u == tile:
                    value = jnp.where(lane >= start + 8 * g + sub, value, 0.0)
                done[g, u] = value
                if u < 2:
                    factor_out[place, 128 * u : 128 * u + 128] = value
                else:
                    work[place, 256:] = value
        after = first + BLOCK
        if after >= 256:
            break
        base = 128 * tile
        panel = jnp.concatenate(
            [jnp.concatenate([done[g, u] for u in tiles], 1) for g in range(groups)], 0
        )
        parts = terms(panel)
        left = left_of(parts, 0)[:, : 256 - base].T
        right = right_of(parts, 0)
        ends = sorted({after, after + BLOCK, max(after, 128), 256})
        for low, high in zip(ends, ends[1:]):
            edge = 128 * (low // 128)
            change = dot(left[low - base : high - base], right[:, edge - base :])
            for u in range(edge // 128, 3):
                old = work[low:high, 128 * u : 128 * u + 128] if first else source(low, high, u)
                at = 128 * u - edge
                work[low:high, 128 * u : 128 * u + 128] = old - change[:, at : at + 128]
    basis_out[:, :128] = work[:128, 256:].T
    basis_out[:, 128:] = work[128:, 256:].T


def factored(cross, sketch):
    vmem = pl.BlockSpec(memory_space=pltpu.VMEM)
    f32 = jnp.float32
    return pl.pallas_call(
        factor_kernel,
        out_shape=(
            jax.ShapeDtypeStruct((128, 256), f32),
            jax.ShapeDtypeStruct((256, 256), f32),
        ),
        in_specs=[vmem, vmem],
        out_specs=(vmem, vmem),
        scratch_shapes=[pltpu.VMEM((256, 384), f32)],
        compiler_params=pltpu.CompilerParams(vmem_limit_bytes=40 << 20),
        name="factored",
    )(cross, sketch)


def on_device(precip, thresholds, bin_index, test_matrix):
    days = precip.shape[0] * lax.axis_size("tm")
    points_total = precip.shape[1] * lax.axis_size(PTS)
    rows = harmonic_basis(days)
    table = np.zeros((lax.axis_size("tm"), 32, precip.shape[0]), np.float32)
    table[:, : len(rows)] = rows.reshape(len(rows), -1, precip.shape[0]).swapaxes(0, 1)
    sketch_t, blocks = gathered(
        precip, table, test_matrix, bin_index.reshape(-1, 128), thresholds, points_total
    )
    return factored(blocks, sketch_t)


def solution(mesh):
    split = Mesh(mesh.devices.reshape(mesh.shape["tm"], 4, 8, 2), ("tm", *PTS))
    return jax.shard_map(
        on_device,
        mesh=split,
        in_specs=(P("tm", PTS), P(), P(PTS), P("tm", None)),
        out_specs=(P(PTS_TM, None), P()),
        check_vma=False,
    )
```
